32 devices in a mesh: gx: 4 (over x, core), gy: 8 (over z, y).
Axes of the slice: x: 2, y: 2, z: 4, core: 2. Of those that a mesh axis runs over, the one named last changes fastest.
Arguments:
- chi: float32 [32, 32, 256], P('gy', 'gx'), may hold values from -6 to 6
- sigma: float32 [32, 32, 256], P('gy', 'gx'), may hold values from 25 to 250
- vertical: float32 [4, 64, 64], replicated, may hold values from -0.75 to 0.75
- kx: float32 [32, 32, 256], P('gy', 'gx'), may hold values from 4 to 120
- ky: float32 [32, 32, 256], P('gy', 'gx'), may hold values from 256 to 7680
Outputs:
- increment: float32 [32, 32, 256], P('gy', 'gx')
The draws below stay inside these ranges and needn't reach their ends.
All inputs are finite; a program needn't handle non-finite values.
Results may differ from the reference program's by a relative error of at most 0.0003.
Values sent between devices are 32-bit elements; how exact they have to be, the bound alone decides.
A program may use at most 64 MiB of HBM per device.

```python
import math
import jax
import jax.numpy as jnp
from jax import lax

F = 4
L = 64
ITERS = 3
FL = 256
NX = 32
NY = 32


def level_of(stream_key, shape, cuts, low, top_value):
    loudness = 1.0
    for axis_at, parts in cuts:
        heights = jax.random.uniform(jax.random.fold_in(jax.random.fold_in(stream_key, 6), axis_at), (parts,), jnp.float32, low / len(cuts), top_value / len(cuts))
        loudness = loudness * jnp.repeat(jnp.exp(heights), shape[axis_at] // parts).reshape((-1,) + (1,) * (len(shape) - 1 - axis_at))
    return loudness


def scatter_about(rng, dims, scale, limit, pieces=(), held_as=jnp.bfloat16):
    values = scale * jax.random.normal(rng, dims, jnp.float32)
    if pieces:
        values = values * level_of(rng, dims, pieces, -0.22, 0.18)
    return jnp.clip(values, -limit, limit).astype(held_as)


def setup_inputs(seed: int = 0) -> dict:
    key_list = jax.random.split(jax.random.key(seed), 6)
    return {
        "chi": scatter_about(key_list[0], (NY, NX, FL), 1.0, 6.0, ((0, 8), (1, 4)), jnp.float32),
        "sigma": jnp.clip(jnp.exp(math.log(250.0) - 2.3025851 * jax.random.uniform(key_list[1], (NY, NX, FL), jnp.float32) ** level_of(key_list[1], (NY, NX, FL), ((0, 8), (1, 4)), -0.2, 0.2)), 25.0, 250.0),
        "vertical": scatter_about(key_list[2], (F, L, L), L ** -0.5, 0.75, (), jnp.float32),
        "kx": jnp.clip(jnp.exp(math.log(120.0) - 3.4011974 * jax.random.uniform(key_list[3], (NY, NX, FL), jnp.float32) ** level_of(key_list[3], (NY, NX, FL), ((0, 8), (1, 4)), -0.2, 0.2)), 4.0, 120.0),
        "ky": jnp.clip(jnp.exp(math.log(7680.0) - 3.4011974 * jax.random.uniform(key_list[4], (NY, NX, FL), jnp.float32) ** level_of(key_list[4], (NY, NX, FL), ((0, 8), (1, 4)), -0.2, 0.2)), 256.0, 7680.0),
    }


def line_solve(values, kleft):
    place = lax.broadcasted_iota(jnp.int32, kleft.shape, 0)
    kleft = jnp.where(place == 0, jnp.zeros_like(kleft), kleft)
    knext = jnp.concatenate([kleft[1:], jnp.zeros_like(kleft[:1])], 0)

    def descend(carry, row):
        excess, eliminated = carry
        conduct, source = row
        pivot = excess + conduct
        new_excess = 1.0 + conduct * excess / pivot
        new_value = source + conduct * eliminated / pivot
        return (new_excess, new_value), (new_excess, new_value)

    start = (jnp.ones_like(values[0]), jnp.zeros_like(values[0]))
    finals, (excesses, reduced) = lax.scan(descend, start, (kleft, values))

    def ascend(carry, row):
        excess, eliminated, conduct = row
        solved_value = (eliminated + conduct * carry) / (excess + conduct)
        return solved_value, solved_value

    ending, solved = lax.scan(ascend, jnp.zeros_like(values[0]), (excesses, reduced, knext), reverse=True)
    return solved


def reference(chi, sigma, vertical, kx, ky):
    fields = vertical.shape[0]
    levels = vertical.shape[1]
    scaled = sigma * chi
    shaped = scaled.reshape(scaled.shape[0], scaled.shape[1], fields, levels)
    mixed = jnp.einsum("yxfl,flk->yxfk", shaped, vertical, precision=lax.Precision.HIGHEST).reshape(scaled.shape)
    current = mixed
    for sweep in range(ITERS):
        current = jnp.swapaxes(line_solve(jnp.swapaxes(current, 0, 1), jnp.swapaxes(kx, 0, 1)), 0, 1)
        current = line_solve(current, ky)
    return current
```

```python
import functools

import jax
import jax.numpy as jnp
from jax import lax
from jax.experimental import pallas as pl
from jax.experimental.pallas import tpu as pltpu
from jax.sharding import PartitionSpec as P

ITERS = 3


def mobius_join(earlier, later):
    top_left = later[0] * earlier[0] + later[1] * earlier[2]
    top_right = later[0] * earlier[1] + later[1] * earlier[3]
    low_left = later[2] * earlier[0] + later[3] * earlier[2]
    low_right = later[2] * earlier[1] + later[3] * earlier[3]
    factor = 1.0 / (top_left + top_right + low_left + low_right)
    return (top_left * factor, top_right * factor, low_left * factor, low_right * factor)


def affine_join(earlier, later):
    return (earlier[0] * later[0], later[0] * earlier[1] + later[1])


def mobius_value(matrix):
    return (matrix[0] + matrix[1]) / (matrix[2] + matrix[3])


def neutral(sample):
    filled = jnp.ones_like(sample[0])
    emptied = jnp.zeros_like(sample[0])
    if len(sample) == 4:
        return (filled, emptied, emptied, filled)
    return (filled, emptied)


def settle(gathered, split, join, position):
    ups = tuple((gathered[:, member_id] for member_id in range(split)))
    downs = tuple((gathered[:, member_id] for member_id in range(split, gathered.shape[1])))
    up_scan = lax.associative_scan(join, ups, axis=0)
    down_scan = lax.associative_scan(join, downs, reverse=True, axis=0)
    up_open = neutral(tuple((member[0] for member in ups)))
    down_open = neutral(tuple((member[0] for member in downs)))
    up_in = tuple(
        (
            lax.dynamic_index_in_dim(jnp.concatenate([anchor[None], member], 0), position, 0, False)
            for anchor, member in zip(up_open, up_scan)
        )
    )
    down_in = tuple(
        (
            lax.dynamic_index_in_dim(
                jnp.concatenate([member, anchor[None]], 0), position + 1, 0, False
            )
            for anchor, member in zip(down_open, down_scan)
        )
    )
    return (up_in, down_in)


def across_x(up_total, down_total, join):
    packed = jnp.stack(up_total + down_total, 0)[None]
    gathered = lax.all_gather(packed, "gx", axis=0, tiled=True)
    return settle(gathered, len(up_total), join, lax.axis_index("gx"))


def across_y(up_total, down_total, join):
    up_in = neutral(up_total)
    down_in = neutral(down_total)
    return (up_in, down_in)


def chain(up_elements, down_elements, join, axis_dim, across):
    span = up_elements[0].shape[axis_dim]
    up_local = lax.associative_scan(join, up_elements, axis=axis_dim)
    down_local = lax.associative_scan(join, down_elements, reverse=True, axis=axis_dim)
    up_total = tuple((lax.index_in_dim(member, span - 1, axis_dim, False) for member in up_local))
    down_total = tuple((lax.index_in_dim(member, 0, axis_dim, False) for member in down_local))
    up_in, down_in = across(up_total, down_total, join)
    up_whole = join(tuple((jnp.expand_dims(member, axis_dim) for member in up_in)), up_local)
    down_whole = join(tuple((jnp.expand_dims(member, axis_dim) for member in down_in)), down_local)
    return (up_in, up_whole, down_in, down_whole)


def open_edge(conduct, axis_dim, position):
    span = conduct.shape[axis_dim]
    place = lax.broadcasted_iota(jnp.int32, conduct.shape, axis_dim) + position * span
    return jnp.where(place == 0, jnp.zeros_like(conduct), conduct)


def operator_terms(kleft, axis_dim, across):
    span = kleft.shape[axis_dim]
    matrices = (1.0 + kleft, kleft, jnp.ones_like(kleft), kleft)
    up_in, up_whole, down_in, down_whole = chain(matrices, matrices, mobius_join, axis_dim, across)
    after = mobius_value(up_whole)
    before = jnp.concatenate(
        [
            jnp.expand_dims(mobius_value(up_in), axis_dim),
            lax.slice_in_dim(after, 0, span - 1, 1, axis_dim),
        ],
        axis_dim,
    )
    behind_whole = mobius_value(down_whole)
    behind = jnp.concatenate(
        [
            lax.slice_in_dim(behind_whole, 1, span, 1, axis_dim),
            jnp.expand_dims(mobius_value(down_in), axis_dim),
        ],
        axis_dim,
    )
    return (kleft / (before + kleft), kleft / (behind + kleft), after + behind - 1.0)


def line_solve(values, terms, axis_dim, across):
    forward_rate, backward_rate, diagonal = terms
    span = values.shape[axis_dim]
    up_in, up_whole, down_in, down_whole = chain(
        (forward_rate, values),
        (backward_rate, backward_rate * values),
        affine_join,
        axis_dim,
        across,
    )
    passed = down_whole[1]
    passed_next = jnp.concatenate(
        [lax.slice_in_dim(passed, 1, span, 1, axis_dim), jnp.expand_dims(down_in[1], axis_dim)],
        axis_dim,
    )
    return (up_whole[1] + passed_next) / diagonal


def to_lines(field, partners):
    row_count = field.shape[0]
    flattened = field.reshape(row_count, -1)
    padding = -flattened.shape[1] % partners
    return jnp.pad(flattened, ((0, 0), (0, padding)))


def from_lines(lines, target_shape):
    return lines[:, : target_shape[1] * target_shape[2]].reshape(target_shape)


def body(chi, sigma, vertical, kx, ky):
    fields = vertical.shape[0]
    levels = vertical.shape[1]
    width = fields * levels
    scaled = sigma * chi
    blocks = (
        jnp.eye(fields, dtype=jnp.float32)[:, None, :, None] * vertical[:, :, None, :]
    ).reshape(width, width)
    mixed = jnp.dot(scaled.reshape(-1, width), blocks, precision=lax.Precision.HIGHEST).reshape(
        scaled.shape
    )
    x_terms = operator_terms(open_edge(kx, 1, lax.axis_index("gx")), 1, across_x)
    partners = lax.axis_size("gy")
    whole_conduct = lax.all_to_all(
        to_lines(ky, partners), "gy", split_axis=1, concat_axis=0, tiled=True
    )
    y_terms = operator_terms(open_edge(whole_conduct, 0, 0), 0, across_y)
    current = mixed
    for sweep in range(ITERS):
        current = line_solve(current, x_terms, 1, across_x)
        whole_lines = lax.all_to_all(
            to_lines(current, partners), "gy", split_axis=1, concat_axis=0, tiled=True
        )
        solved = line_solve(whole_lines, y_terms, 0, across_y)
        current = from_lines(
            lax.all_to_all(solved, "gy", split_axis=0, concat_axis=1, tiled=True), current.shape
        )
    return current


LANES = 128
SUBLANES = 8


def channels_fit(shape, split_x, split_y):
    rows, span, width = shape
    return (
        span == SUBLANES
        and rows * span * split_x == LANES
        and split_x >= 3
        and width == SUBLANES * split_x * split_y
        and rows & (rows - 1) == 0
        and split_x & (split_x - 1) == 0
        and split_y & (split_y - 1) == 0
    )


def reduction_rates(kleft, length, below, above):
    excess = jnp.ones_like(kleft)
    west = kleft
    east = above(kleft, 1)
    rates = []
    stride = 1
    while stride < length:
        inverse = 1.0 / (excess + west + east)
        from_below = west * below(inverse, stride)
        from_above = east * above(inverse, stride)
        excess = excess + from_below * below(excess, stride) + from_above * above(excess, stride)
        west = from_below * below(west, stride)
        east = from_above * above(east, stride)
        rates.append((stride, from_below, from_above))
        stride *= 2
    return rates, 1.0 / excess


def reduced_solve(values, operator, below, above):
    rates, inverse = operator
    for stride, from_below, from_above in rates:
        values = values + from_below * below(values, stride) + from_above * above(values, stride)
    return values * inverse


def channel_kernel(
    split_x,
    split_y,
    chi_ref,
    sigma_ref,
    vertical_ref,
    kx_ref,
    ky_ref,
    out_ref,
    staged,
    sent,
    got,
    solved,
    back,
    turned,
    send_sem,
    recv_sem,
    back_send_sem,
    back_recv_sem,
):
    rows, span, width = chi_ref.shape
    fields, levels, _ = vertical_ref.shape
    count = split_x * split_y
    length_x = split_x * span
    length_y = split_y * rows
    gx, gy = (lax.axis_index("gx"), lax.axis_index("gy"))
    me = gy * split_x + gx

    def peer_at(step):
        peer = lax.rem(me + step, count)
        return peer, peer // split_x, lax.rem(peer, split_x)

    barrier = pltpu.get_barrier_semaphore()
    for step in range(1, count):
        _, peer_y, peer_x = peer_at(step)
        pl.semaphore_signal(
            barrier,
            inc=1,
            device_id={"gx": peer_x, "gy": peer_y},
            device_id_type=pl.DeviceIdType.MESH,
        )

    scaled = (sigma_ref[...] * chi_ref[...]).reshape(rows * span, width)
    mixed = jnp.concatenate(
        [
            jnp.dot(
                scaled[:, f * levels : (f + 1) * levels],
                vertical_ref[f],
                precision=lax.Precision.HIGHEST,
                preferred_element_type=jnp.float32,
            )
            for f in range(fields)
        ],
        1,
    )

    def place(turn, row, tile):
        block = row * split_x + lax.rem(gx + turn, split_x)
        staged[pl.ds(pl.multiple_of(block * span, span), span), :] = tile

    for row in range(rows):
        place(0, row, mixed[row * span : (row + 1) * span])
        place(1, row, kx_ref[row])
        place(2, row, ky_ref[row])
        for turn in range(3, split_x):
            place(turn, row, jnp.zeros((span, width), jnp.float32))
    sent[...] = staged[...].T.reshape(sent.shape)

    pl.semaphore_wait(barrier, count - 1)
    for step in range(1, count):
        peer, peer_y, peer_x = peer_at(step)
        pltpu.make_async_remote_copy(
            src_ref=sent.at[peer],
            dst_ref=got.at[me],
            send_sem=send_sem,
            recv_sem=recv_sem,
            device_id={"gx": peer_x, "gy": peer_y},
            device_id_type=pl.DeviceIdType.MESH,
        ).start()
    got[me] = sent[me]
    others = pl.ds(0, count - 1)
    pltpu.make_async_copy(got.at[others], got.at[others], recv_sem).wait()

    lane = lax.broadcasted_iota(jnp.int32, (split_y * SUBLANES, LANES), 1)
    tile_row = lax.broadcasted_iota(jnp.int32, (split_y * SUBLANES, LANES), 0)
    cell_x = lane % length_x
    block_x = cell_x // span
    tiles = got[...].reshape(split_y, split_x, SUBLANES, LANES)
    sources = [tiles[:, g].reshape(split_y * SUBLANES, LANES) for g in range(split_x)]

    def collect(turn):
        whole = sources[0]
        for g in range(1, split_x):
            whole = jnp.where(block_x == (g + turn) % split_x, sources[g], whole)
        if turn:
            ahead = pltpu.roll(whole, LANES - turn * span, 1)
            wrapped = pltpu.roll(whole, length_x - turn * span, 1)
            whole = jnp.where(cell_x < length_x - turn * span, ahead, wrapped)
        return whole

    def tiles_on(values, tiles_by):
        moved = (tiles_by % split_y) * SUBLANES
        if moved == 0:
            return values
        return jnp.concatenate([values[-moved:], values[:-moved]], 0)

    def below_x(values, stride):
        return pltpu.roll(values, stride, 1)

    def above_x(values, stride):
        return pltpu.roll(values, LANES - stride, 1)

    def below_y(values, stride):
        if stride >= rows:
            return tiles_on(values, stride // rows)
        lanes = stride * length_x
        turned_by = pltpu.roll(values, lanes, 1)
        return jnp.where(lane < lanes, tiles_on(turned_by, 1), turned_by)

    def above_y(values, stride):
        if stride >= rows:
            return tiles_on(values, -(stride // rows))
        lanes = stride * length_x
        turned_by = pltpu.roll(values, LANES - lanes, 1)
        return jnp.where(lane >= LANES - lanes, tiles_on(turned_by, -1), turned_by)

    field = collect(0)
    west = jnp.where(cell_x == 0, 0.0, collect(1))
    south = jnp.where((tile_row < SUBLANES) & (lane < length_x), 0.0, collect(2))
    x_operator = reduction_rates(west, length_x, below_x, above_x)
    y_operator = reduction_rates(south, length_y, below_y, above_y)
    for sweep in range(ITERS):
        field = reduced_solve(field, x_operator, below_x, above_x)
        field = reduced_solve(field, y_operator, below_y, above_y)
    solved[...] = field.reshape(solved.shape)

    for step in range(1, count):
        peer, peer_y, peer_x = peer_at(step)
        pltpu.make_async_remote_copy(
            src_ref=solved.at[peer_y],
            dst_ref=back.at[me],
            send_sem=back_send_sem,
            recv_sem=back_recv_sem,
            device_id={"gx": peer_x, "gy": peer_y},
            device_id_type=pl.DeviceIdType.MESH,
        ).start()
    back[me] = solved[gy]
    pltpu.make_async_copy(back.at[others], back.at[others], back_recv_sem).wait()
    turned[...] = back[...].reshape(count * SUBLANES, LANES).T
    for row in range(rows):
        start = pl.multiple_of((row * split_x + gx) * span, span)
        out_ref[row] = turned[pl.ds(start, span), :]
    pltpu.make_async_copy(sent.at[others], sent.at[others], send_sem).wait()
    pltpu.make_async_copy(back.at[others], back.at[others], back_send_sem).wait()


def channel_body(split_x, split_y, chi, sigma, vertical, kx, ky):
    rows, span, width = chi.shape
    count = split_x * split_y
    whole = pl.BlockSpec(memory_space=pltpu.VMEM)
    return pl.pallas_call(
        functools.partial(channel_kernel, split_x, split_y),
        out_shape=jax.ShapeDtypeStruct(chi.shape, jnp.float32),
        in_specs=[whole] * 5,
        out_specs=whole,
        scratch_shapes=[
            pltpu.VMEM((LANES, width), jnp.float32),
            pltpu.VMEM((count, SUBLANES, LANES), jnp.float32),
            pltpu.VMEM((count, SUBLANES, LANES), jnp.float32),
            pltpu.VMEM((split_y, SUBLANES, LANES), jnp.float32),
            pltpu.VMEM((count, SUBLANES, LANES), jnp.float32),
            pltpu.VMEM((LANES, width), jnp.float32),
            pltpu.SemaphoreType.DMA,
            pltpu.SemaphoreType.DMA,
            pltpu.SemaphoreType.DMA,
            pltpu.SemaphoreType.DMA,
        ],
        compiler_params=pltpu.CompilerParams(collective_id=0, has_side_effects=True),
        name="channel_lines",
    )(chi, sigma, vertical, kx, ky)


def solution(mesh):
    split_x, split_y = (mesh.shape["gx"], mesh.shape["gy"])

    def chosen(chi, sigma, vertical, kx, ky):
        if channels_fit(chi.shape, split_x, split_y):
            return channel_body(split_x, split_y, chi, sigma, vertical, kx, ky)
        return body(chi, sigma, vertical, kx, ky)


    placed = (
        P("gy", "gx", None),
        P("gy", "gx", None),
        P(),
        P("gy", "gx", None),
        P("gy", "gx", None),
    )
    return jax.shard_map(
        chosen, mesh=mesh, in_specs=placed, out_specs=P("gy", "gx", None), check_vma=False
    )
```

```python
import functools

import jax
import jax.numpy as jnp
from jax import lax
from jax.experimental import pallas as pl
from jax.experimental.pallas import tpu as pltpu
from jax.sharding import PartitionSpec as P

ITERS = 3


def mobius_join(earlier, later):
    top_left = later[0] * earlier[0] + later[1] * earlier[2]
    top_right = later[0] * earlier[1] + later[1] * earlier[3]
    low_left = later[2] * earlier[0] + later[3] * earlier[2]
    low_right = later[2] * earlier[1] + later[3] * earlier[3]
    factor = 1.0 / (top_left + top_right + low_left + low_right)
    return (top_left * factor, top_right * factor, low_left * factor, low_right * factor)


def affine_join(earlier, later):
    return (earlier[0] * later[0], later[0] * earlier[1] + later[1])


def mobius_value(matrix):
    return (matrix[0] + matrix[1]) / (matrix[2] + matrix[3])


def neutral(sample):
    filled = jnp.ones_like(sample[0])
    emptied = jnp.zeros_like(sample[0])
    if len(sample) == 4:
        return (filled, emptied, emptied, filled)
    return (filled, emptied)


def settle(gathered, split, join, position):
    ups = tuple((gathered[:, member_id] for member_id in range(split)))
    downs = tuple((gathered[:, member_id] for member_id in range(split, gathered.shape[1])))
    up_scan = lax.associative_scan(join, ups, axis=0)
    down_scan = lax.associative_scan(join, downs, reverse=True, axis=0)
    up_open = neutral(tuple((member[0] for member in ups)))
    down_open = neutral(tuple((member[0] for member in downs)))
    up_in = tuple(
        (
            lax.dynamic_index_in_dim(jnp.concatenate([anchor[None], member], 0), position, 0, False)
            for anchor, member in zip(up_open, up_scan)
        )
    )
    down_in = tuple(
        (
            lax.dynamic_index_in_dim(
                jnp.concatenate([member, anchor[None]], 0), position + 1, 0, False
            )
            for anchor, member in zip(down_open, down_scan)
        )
    )
    return (up_in, down_in)


def across_x(up_total, down_total, join):
    packed = jnp.stack(up_total + down_total, 0)[None]
    gathered = lax.all_gather(packed, "gx", axis=0, tiled=True)
    return settle(gathered, len(up_total), join, lax.axis_index("gx"))


def across_y(up_total, down_total, join):
    up_in = neutral(up_total)
    down_in = neutral(down_total)
    return (up_in, down_in)


def chain(up_elements, down_elements, join, axis_dim, across):
    span = up_elements[0].shape[axis_dim]
    up_local = lax.associative_scan(join, up_elements, axis=axis_dim)
    down_local = lax.associative_scan(join, down_elements, reverse=True, axis=axis_dim)
    up_total = tuple((lax.index_in_dim(member, span - 1, axis_dim, False) for member in up_local))
    down_total = tuple((lax.index_in_dim(member, 0, axis_dim, False) for member in down_local))
    up_in, down_in = across(up_total, down_total, join)
    up_whole = join(tuple((jnp.expand_dims(member, axis_dim) for member in up_in)), up_local)
    down_whole = join(tuple((jnp.expand_dims(member, axis_dim) for member in down_in)), down_local)
    return (up_in, up_whole, down_in, down_whole)


def open_edge(conduct, axis_dim, position):
    span = conduct.shape[axis_dim]
    place = lax.broadcasted_iota(jnp.int32, conduct.shape, axis_dim) + position * span
    return jnp.where(place == 0, jnp.zeros_like(conduct), conduct)


def operator_terms(kleft, axis_dim, across):
    span = kleft.shape[axis_dim]
    matrices = (1.0 + kleft, kleft, jnp.ones_like(kleft), kleft)
    up_in, up_whole, down_in, down_whole = chain(matrices, matrices, mobius_join, axis_dim, across)
    after = mobius_value(up_whole)
    before = jnp.concatenate(
        [
            jnp.expand_dims(mobius_value(up_in), axis_dim),
            lax.slice_in_dim(after, 0, span - 1, 1, axis_dim),
        ],
        axis_dim,
    )
    behind_whole = mobius_value(down_whole)
    behind = jnp.concatenate(
        [
            lax.slice_in_dim(behind_whole, 1, span, 1, axis_dim),
            jnp.expand_dims(mobius_value(down_in), axis_dim),
        ],
        axis_dim,
    )
    return (kleft / (before + kleft), kleft / (behind + kleft), after + behind - 1.0)


def line_solve(values, terms, axis_dim, across):
    forward_rate, backward_rate, diagonal = terms
    span = values.shape[axis_dim]
    up_in, up_whole, down_in, down_whole = chain(
        (forward_rate, values),
        (backward_rate, backward_rate * values),
        affine_join,
        axis_dim,
        across,
    )
    passed = down_whole[1]
    passed_next = jnp.concatenate(
        [lax.slice_in_dim(passed, 1, span, 1, axis_dim), jnp.expand_dims(down_in[1], axis_dim)],
        axis_dim,
    )
    return (up_whole[1] + passed_next) / diagonal


def to_lines(field, partners):
    row_count = field.shape[0]
    flattened = field.reshape(row_count, -1)
    padding = -flattened.shape[1] % partners
    return jnp.pad(flattened, ((0, 0), (0, padding)))


def from_lines(lines, target_shape):
    return lines[:, : target_shape[1] * target_shape[2]].reshape(target_shape)


def body(chi, sigma, vertical, kx, ky):
    fields = vertical.shape[0]
    levels = vertical.shape[1]
    width = fields * levels
    scaled = sigma * chi
    blocks = (
        jnp.eye(fields, dtype=jnp.float32)[:, None, :, None] * vertical[:, :, None, :]
    ).reshape(width, width)
    mixed = jnp.dot(scaled.reshape(-1, width), blocks, precision=lax.Precision.HIGHEST).reshape(
        scaled.shape
    )
    x_terms = operator_terms(open_edge(kx, 1, lax.axis_index("gx")), 1, across_x)
    partners = lax.axis_size("gy")
    whole_conduct = lax.all_to_all(
        to_lines(ky, partners), "gy", split_axis=1, concat_axis=0, tiled=True
    )
    y_terms = operator_terms(open_edge(whole_conduct, 0, 0), 0, across_y)
    current = mixed
    for sweep in range(ITERS):
        current = line_solve(current, x_terms, 1, across_x)
        whole_lines = lax.all_to_all(
            to_lines(current, partners), "gy", split_axis=1, concat_axis=0, tiled=True
        )
        solved = line_solve(whole_lines, y_terms, 0, across_y)
        current = from_lines(
            lax.all_to_all(solved, "gy", split_axis=0, concat_axis=1, tiled=True), current.shape
        )
    return current


LANES = 128
SUBLANES = 8


def channels_fit(shape, fields, split_x, split_y):
    rows, span, width = shape
    return (
        span == SUBLANES
        and rows * span * split_x == LANES
        and fields == split_x
        and SUBLANES % split_x == 0
        and width == SUBLANES * split_x * split_y
        and rows & (rows - 1) == 0
        and split_x & (split_x - 1) == 0
        and split_y & (split_y - 1) == 0
    )


def reduction_rates(kleft, length, below, above):
    excess = jnp.ones_like(kleft)
    west = kleft
    east = above(kleft, 1)
    rates = []
    stride = 1
    while stride < length:
        inverse = 1.0 / (excess + west + east)
        from_below = west * below(inverse, stride)
        from_above = east * above(inverse, stride)
        excess = excess + from_below * below(excess, stride) + from_above * above(excess, stride)
        west = from_below * below(west, stride)
        east = from_above * above(east, stride)
        rates.append((stride, from_below, from_above))
        stride *= 2
    return rates, 1.0 / excess


def reduced_solve(values, operator, below, above):
    rates, inverse = operator
    for stride, from_below, from_above in rates:
        values = values + from_below * below(values, stride) + from_above * above(values, stride)
    return values * inverse


def swap_blocks(values, span, split_x):
    row = lax.broadcasted_iota(jnp.int32, values.shape, 0)
    lane = lax.broadcasted_iota(jnp.int32, values.shape, 1)
    down, along = (SUBLANES // split_x, span)
    while down < SUBLANES:
        row_bit = (row // down) % 2
        lane_bit = (lane // along) % 2
        later = pltpu.roll(pltpu.roll(values, along, 1), values.shape[0] - down, 0)
        earlier = pltpu.roll(pltpu.roll(values, LANES - along, 1), down, 0)
        values = jnp.where(row_bit == lane_bit, values, jnp.where(lane_bit == 1, later, earlier))
        down, along = (down * 2, along * 2)
    return values


def channel_kernel(
    split_x,
    split_y,
    chi_hbm,
    sigma_hbm,
    vertical_hbm,
    kx_hbm,
    ky_hbm,
    out_ref,
    chi_ref,
    sigma_ref,
    vertical_ref,
    kx_ref,
    ky_ref,
    sent_k,
    got_k,
    sent_f,
    got_f,
    solved,
    back,
    load_sems,
    k_sems,
    f_sems,
    back_sems,
):
    rows, span, width = chi_ref.shape
    fields, levels, _ = vertical_ref.shape
    count = split_x * split_y
    length_x = split_x * span
    length_y = split_y * rows
    tall = split_y * SUBLANES
    gx, gy = (lax.axis_index("gx"), lax.axis_index("gy"))
    me = gy * split_x + gx

    loads = [
        pltpu.make_async_copy(source, target, load_sems.at[number])
        for number, (source, target) in enumerate(
            (
                (kx_hbm, kx_ref),
                (ky_hbm, ky_ref),
                (chi_hbm, chi_ref),
                (sigma_hbm, sigma_ref),
                (vertical_hbm, vertical_ref),
            )
        )
    ]
    for load in loads:
        load.start()

    partners_x = [lax.bitwise_xor(gx, jnp.int32(step)) for step in range(split_x)]
    partners_y = [lax.bitwise_xor(gy, jnp.int32(step)) for step in range(split_y)]
    partners = [
        (partners_x[step_x], partners_y[step_y])
        for step_y in reversed(range(split_y))
        for step_x in range(split_x)
        if step_x or step_y
    ]

    barrier = pltpu.get_barrier_semaphore()
    for peer_x, peer_y in partners:
        pl.semaphore_signal(
            barrier,
            inc=1,
            device_id={"gx": peer_x, "gy": peer_y},
            device_id_type=pl.DeviceIdType.MESH,
        )

    def send_all(source, target, sems):
        for peer_x, peer_y in partners:
            pltpu.make_async_remote_copy(
                src_ref=source(peer_y * split_x + peer_x),
                dst_ref=target(me),
                send_sem=sems.at[0],
                recv_sem=sems.at[1],
                device_id={"gx": peer_x, "gy": peer_y},
                device_id_type=pl.DeviceIdType.MESH,
            ).start()

    others = pl.ds(0, count - 1)
    loads[0].wait()
    loads[1].wait()
    group = width // split_x
    conducts = jnp.concatenate(
        [
            jnp.concatenate([ref[row][:, h * group : (h + 1) * group] for ref in (kx_ref, ky_ref)], 1)
            for row in range(rows)
            for h in range(split_x)
        ],
        0,
    )
    sent_k[...] = conducts.T.reshape(sent_k.shape)
    pl.semaphore_wait(barrier, count - 1)
    send_all(lambda at: sent_k.at[:, at], lambda at: got_k.at[:, at], k_sems)

    for load in loads[2:]:
        load.wait()
    scaled = (sigma_ref[...] * chi_ref[...]).reshape(rows * span, width)
    mixed = [
        jnp.dot(
            scaled[:, f * levels : (f + 1) * levels],
            vertical_ref[f],
            precision=lax.Precision.HIGHEST,
            preferred_element_type=jnp.float32,
        )
        for f in range(fields)
    ]
    stacked = jnp.concatenate(
        [mixed[f][row * span : (row + 1) * span] for row in range(rows) for f in range(fields)], 0
    )
    sent_f[...] = stacked.T.reshape(sent_f.shape)
    send_all(lambda at: sent_f.at[at], lambda at: got_f.at[at], f_sems)
    got_k[:, me] = sent_k[:, me]
    got_f[me] = sent_f[me]

    lane = lax.broadcasted_iota(jnp.int32, (tall, LANES), 1)
    tile_row = lax.broadcasted_iota(jnp.int32, (tall, LANES), 0)
    cell_x = lane % length_x

    def tiles_on(values, tiles_by):
        moved = (tiles_by % split_y) * SUBLANES
        if moved == 0:
            return values
        return jnp.concatenate([values[-moved:], values[:-moved]], 0)

    def below_x(values, stride):
        return pltpu.roll(values, stride, 1)

    def above_x(values, stride):
        return pltpu.roll(values, LANES - stride, 1)

    def below_y(values, stride):
        if stride >= rows:
            return tiles_on(values, stride // rows)
        lanes = stride * length_x
        turned_by = pltpu.roll(values, lanes, 1)
        return jnp.where(lane < lanes, tiles_on(turned_by, 1), turned_by)

    def above_y(values, stride):
        if stride >= rows:
            return tiles_on(values, -(stride // rows))
        lanes = stride * length_x
        turned_by = pltpu.roll(values, LANES - lanes, 1)
        return jnp.where(lane >= LANES - lanes, tiles_on(turned_by, -1), turned_by)

    pltpu.make_async_copy(got_k.at[:, others], got_k.at[:, others], k_sems.at[1]).wait()
    west = swap_blocks(got_k[0].reshape(tall, LANES), span, split_x)
    south = swap_blocks(got_k[1].reshape(tall, LANES), span, split_x)
    west = jnp.where(cell_x == 0, 0.0, west)
    south = jnp.where((tile_row < SUBLANES) & (lane < length_x), 0.0, south)
    x_operator = reduction_rates(west, length_x, below_x, above_x)
    y_operator = reduction_rates(south, length_y, below_y, above_y)
    pltpu.make_async_copy(got_f.at[others], got_f.at[others], f_sems.at[1]).wait()
    field = swap_blocks(got_f[...].reshape(tall, LANES), span, split_x)
    for sweep in range(ITERS):
        field = reduced_solve(field, x_operator, below_x, above_x)
        field = reduced_solve(field, y_operator, below_y, above_y)
    solved[...] = swap_blocks(field, span, split_x).reshape(solved.shape)
    send_all(lambda at: solved.at[at], lambda at: back.at[at], back_sems)
    back[me] = solved[me]
    pltpu.make_async_copy(back.at[others], back.at[others], back_sems.at[1]).wait()
    turned = back[...].reshape(tall, LANES).T
    for row in range(rows):
        out_ref[row] = jnp.concatenate(
            [
                turned[(row * split_x + h) * span : (row * split_x + h + 1) * span]
                for h in range(split_x)
            ],
            1,
        )
    pltpu.make_async_copy(sent_k.at[:, others], sent_k.at[:, others], k_sems.at[0]).wait()
    pltpu.make_async_copy(sent_f.at[others], sent_f.at[others], f_sems.at[0]).wait()
    pltpu.make_async_copy(solved.at[others], solved.at[others], back_sems.at[0]).wait()


def channel_body(split_x, split_y, chi, sigma, vertical, kx, ky):
    count = split_x * split_y
    share = SUBLANES // split_x
    block = pltpu.VMEM(chi.shape, jnp.float32)
    packed = pltpu.VMEM((count, share, LANES), jnp.float32)
    packed_pair = pltpu.VMEM((2, count, share, LANES), jnp.float32)
    return pl.pallas_call(
        functools.partial(channel_kernel, split_x, split_y),
        out_shape=pltpu.VMEM(chi.shape, jnp.float32),
        in_specs=[pl.BlockSpec(memory_space=pl.ANY)] * 5,
        out_specs=pl.BlockSpec(memory_space=pltpu.VMEM),
        scratch_shapes=[
            block,
            block,
            pltpu.VMEM(vertical.shape, jnp.float32),
            block,
            block,
            packed_pair,
            packed_pair,
            packed,
            packed,
            packed,
            packed,
            pltpu.SemaphoreType.DMA((5,)),
            pltpu.SemaphoreType.DMA((2,)),
            pltpu.SemaphoreType.DMA((2,)),
            pltpu.SemaphoreType.DMA((2,)),
        ],
        compiler_params=pltpu.CompilerParams(collective_id=0, has_side_effects=True),
        name="channel_lines",
    )(chi, sigma, vertical, kx, ky)


def solution(mesh):
    split_x, split_y = (mesh.shape["gx"], mesh.shape["gy"])

    def chosen(chi, sigma, vertical, kx, ky):
        if channels_fit(chi.shape, vertical.shape[0], split_x, split_y):
            return channel_body(split_x, split_y, chi, sigma, vertical, kx, ky)
        return body(chi, sigma, vertical, kx, ky)


    placed = (
        P("gy", "gx", None),
        P("gy", "gx", None),
        P(),
        P("gy", "gx", None),
        P("gy", "gx", None),
    )
    return jax.shard_map(
        chosen, mesh=mesh, in_specs=placed, out_specs=P("gy", "gx", None), check_vma=False
    )
```

```python
import functools

import jax
import jax.numpy as jnp
from jax import lax
from jax.experimental import pallas as pl
from jax.experimental.pallas import tpu as pltpu
from jax.sharding import PartitionSpec as P

ITERS = 3


def mobius_join(earlier, later):
    top_left = later[0] * earlier[0] + later[1] * earlier[2]
    top_right = later[0] * earlier[1] + later[1] * earlier[3]
    low_left = later[2] * earlier[0] + later[3] * earlier[2]
    low_right = later[2] * earlier[1] + later[3] * earlier[3]
    factor = 1.0 / (top_left + top_right + low_left + low_right)
    return (top_left * factor, top_right * factor, low_left * factor, low_right * factor)


def affine_join(earlier, later):
    return (earlier[0] * later[0], later[0] * earlier[1] + later[1])


def mobius_value(matrix):
    return (matrix[0] + matrix[1]) / (matrix[2] + matrix[3])


def neutral(sample):
    filled = jnp.ones_like(sample[0])
    emptied = jnp.zeros_like(sample[0])
    if len(sample) == 4:
        return (filled, emptied, emptied, filled)
    return (filled, emptied)


def settle(gathered, split, join, position):
    ups = tuple((gathered[:, member_id] for member_id in range(split)))
    downs = tuple((gathered[:, member_id] for member_id in range(split, gathered.shape[1])))
    up_scan = lax.associative_scan(join, ups, axis=0)
    down_scan = lax.associative_scan(join, downs, reverse=True, axis=0)
    up_open = neutral(tuple((member[0] for member in ups)))
    down_open = neutral(tuple((member[0] for member in downs)))
    up_in = tuple(
        (
            lax.dynamic_index_in_dim(jnp.concatenate([anchor[None], member], 0), position, 0, False)
            for anchor, member in zip(up_open, up_scan)
        )
    )
    down_in = tuple(
        (
            lax.dynamic_index_in_dim(
                jnp.concatenate([member, anchor[None]], 0), position + 1, 0, False
            )
            for anchor, member in zip(down_open, down_scan)
        )
    )
    return (up_in, down_in)


def across_x(up_total, down_total, join):
    packed = jnp.stack(up_total + down_total, 0)[None]
    gathered = lax.all_gather(packed, "gx", axis=0, tiled=True)
    return settle(gathered, len(up_total), join, lax.axis_index("gx"))


def across_y(up_total, down_total, join):
    up_in = neutral(up_total)
    down_in = neutral(down_total)
    return (up_in, down_in)


def chain(up_elements, down_elements, join, axis_dim, across):
    span = up_elements[0].shape[axis_dim]
    up_local = lax.associative_scan(join, up_elements, axis=axis_dim)
    down_local = lax.associative_scan(join, down_elements, reverse=True, axis=axis_dim)
    up_total = tuple((lax.index_in_dim(member, span - 1, axis_dim, False) for member in up_local))
    down_total = tuple((lax.index_in_dim(member, 0, axis_dim, False) for member in down_local))
    up_in, down_in = across(up_total, down_total, join)
    up_whole = join(tuple((jnp.expand_dims(member, axis_dim) for member in up_in)), up_local)
    down_whole = join(tuple((jnp.expand_dims(member, axis_dim) for member in down_in)), down_local)
    return (up_in, up_whole, down_in, down_whole)


def open_edge(conduct, axis_dim, position):
    span = conduct.shape[axis_dim]
    place = lax.broadcasted_iota(jnp.int32, conduct.shape, axis_dim) + position * span
    return jnp.where(place == 0, jnp.zeros_like(conduct), conduct)


def operator_terms(kleft, axis_dim, across):
    span = kleft.shape[axis_dim]
    matrices = (1.0 + kleft, kleft, jnp.ones_like(kleft), kleft)
    up_in, up_whole, down_in, down_whole = chain(matrices, matrices, mobius_join, axis_dim, across)
    after = mobius_value(up_whole)
    before = jnp.concatenate(
        [
            jnp.expand_dims(mobius_value(up_in), axis_dim),
            lax.slice_in_dim(after, 0, span - 1, 1, axis_dim),
        ],
        axis_dim,
    )
    behind_whole = mobius_value(down_whole)
    behind = jnp.concatenate(
        [
            lax.slice_in_dim(behind_whole, 1, span, 1, axis_dim),
            jnp.expand_dims(mobius_value(down_in), axis_dim),
        ],
        axis_dim,
    )
    return (kleft / (before + kleft), kleft / (behind + kleft), after + behind - 1.0)


def line_solve(values, terms, axis_dim, across):
    forward_rate, backward_rate, diagonal = terms
    span = values.shape[axis_dim]
    up_in, up_whole, down_in, down_whole = chain(
        (forward_rate, values),
        (backward_rate, backward_rate * values),
        affine_join,
        axis_dim,
        across,
    )
    passed = down_whole[1]
    passed_next = jnp.concatenate(
        [lax.slice_in_dim(passed, 1, span, 1, axis_dim), jnp.expand_dims(down_in[1], axis_dim)],
        axis_dim,
    )
    return (up_whole[1] + passed_next) / diagonal


def to_lines(field, partners):
    row_count = field.shape[0]
    flattened = field.reshape(row_count, -1)
    padding = -flattened.shape[1] % partners
    return jnp.pad(flattened, ((0, 0), (0, padding)))


def from_lines(lines, target_shape):
    return lines[:, : target_shape[1] * target_shape[2]].reshape(target_shape)


def body(chi, sigma, vertical, kx, ky):
    fields = vertical.shape[0]
    levels = vertical.shape[1]
    width = fields * levels
    scaled = sigma * chi
    blocks = (
        jnp.eye(fields, dtype=jnp.float32)[:, None, :, None] * vertical[:, :, None, :]
    ).reshape(width, width)
    mixed = jnp.dot(scaled.reshape(-1, width), blocks, precision=lax.Precision.HIGHEST).reshape(
        scaled.shape
    )
    x_terms = operator_terms(open_edge(kx, 1, lax.axis_index("gx")), 1, across_x)
    partners = lax.axis_size("gy")
    whole_conduct = lax.all_to_all(
        to_lines(ky, partners), "gy", split_axis=1, concat_axis=0, tiled=True
    )
    y_terms = operator_terms(open_edge(whole_conduct, 0, 0), 0, across_y)
    current = mixed
    for sweep in range(ITERS):
        current = line_solve(current, x_terms, 1, across_x)
        whole_lines = lax.all_to_all(
            to_lines(current, partners), "gy", split_axis=1, concat_axis=0, tiled=True
        )
        solved = line_solve(whole_lines, y_terms, 0, across_y)
        current = from_lines(
            lax.all_to_all(solved, "gy", split_axis=0, concat_axis=1, tiled=True), current.shape
        )
    return current


LANES = 128
SUBLANES = 8


def channels_fit(shape, fields, split_x, split_y):
    rows, span, width = shape
    return (
        span == SUBLANES
        and rows * span * split_x == LANES
        and fields == split_x
        and SUBLANES % split_x == 0
        and width == SUBLANES * split_x * split_y
        and rows & (rows - 1) == 0
        and split_x & (split_x - 1) == 0
        and split_y & (split_y - 1) == 0
    )


def cyclic_reduction(kleft, length, at, paired):
    excess = jnp.ones_like(kleft)
    west = kleft
    east = at(kleft, 1)
    levels = []
    stride = 1
    while stride < length:
        inverse = 1.0 / (excess + west + east)
        from_west = west * at(inverse, -stride)
        from_east = east * at(inverse, stride)
        excess = excess + from_west * at(excess, -stride) + from_east * at(excess, stride)
        west = from_west * at(west, -stride)
        east = from_east * at(east, stride)
        levels.append((stride, from_west, from_east))
        stride *= 2
    steps = []
    while levels:
        near, west_near, east_near = levels.pop(0)
        if levels and paired(near):
            far, west_far, east_far = levels.pop(0)
            steps.append(
                (
                    (-near, west_near + west_far * at(east_near, -far)),
                    (near, east_near + east_far * at(west_near, far)),
                    (-far, west_far),
                    (far, east_far),
                    (-near - far, west_far * at(west_near, -far)),
                    (near + far, east_far * at(east_near, far)),
                )
            )
        else:
            steps.append(((-near, west_near), (near, east_near)))
    return steps, 1.0 / excess


def reduced_solve(values, operator, at):
    steps, inverse = operator
    for taps in steps:
        terms = [coefficient * at(values, offset) for offset, coefficient in taps]
        terms = [first + second for first, second in zip(terms[::2], terms[1::2])]
        values = (values + terms[0]) + sum(terms[2:], terms[1]) if terms[1:] else values + terms[0]
    return values * inverse


def swap_blocks(values, span, split_x):
    row = lax.broadcasted_iota(jnp.int32, values.shape, 0)
    lane = lax.broadcasted_iota(jnp.int32, values.shape, 1)
    down, along = (SUBLANES // split_x, span)
    while down < SUBLANES:
        row_bit = (row // down) % 2
        lane_bit = (lane // along) % 2
        later = pltpu.roll(pltpu.roll(values, along, 1), values.shape[0] - down, 0)
        earlier = pltpu.roll(pltpu.roll(values, LANES - along, 1), down, 0)
        values = jnp.where(row_bit == lane_bit, values, jnp.where(lane_bit == 1, later, earlier))
        down, along = (down * 2, along * 2)
    return values


def channel_kernel(
    split_x,
    split_y,
    chi_hbm,
    sigma_hbm,
    vertical_hbm,
    kx_hbm,
    ky_hbm,
    out_ref,
    chi_ref,
    sigma_ref,
    vertical_ref,
    kx_ref,
    ky_ref,
    sent_k,
    got_k,
    sent_f,
    got_f,
    solved,
    back,
    load_sems,
    k_sems,
    f_sems,
    back_sems,
):
    rows, span, width = chi_ref.shape
    fields, levels, _ = vertical_ref.shape
    count = split_x * split_y
    length_x = split_x * span
    length_y = split_y * rows
    tall = split_y * SUBLANES
    gx, gy = (lax.axis_index("gx"), lax.axis_index("gy"))
    me = gy * split_x + gx

    loads = [
        pltpu.make_async_copy(source, target, load_sems.at[number])
        for number, (source, target) in enumerate(
            (
                (kx_hbm, kx_ref),
                (ky_hbm, ky_ref),
                (chi_hbm, chi_ref),
                (sigma_hbm, sigma_ref),
                (vertical_hbm, vertical_ref),
            )
        )
    ]
    for load in loads:
        load.start()

    partners_x = [lax.bitwise_xor(gx, jnp.int32(step)) for step in range(split_x)]
    partners_y = [lax.bitwise_xor(gy, jnp.int32(step)) for step in range(split_y)]
    partners = [
        (partners_x[step_x], partners_y[step_y])
        for step_y in reversed(range(split_y))
        for step_x in range(split_x)
        if step_x or step_y
    ]

    barrier = pltpu.get_barrier_semaphore()
    for peer_x, peer_y in partners:
        pl.semaphore_signal(
            barrier,
            inc=1,
            device_id={"gx": peer_x, "gy": peer_y},
            device_id_type=pl.DeviceIdType.MESH,
        )

    def send_all(source, target, sems):
        for peer_x, peer_y in partners:
            pltpu.make_async_remote_copy(
                src_ref=source(peer_y * split_x + peer_x),
                dst_ref=target(me),
                send_sem=sems.at[0],
                recv_sem=sems.at[1],
                device_id={"gx": peer_x, "gy": peer_y},
                device_id_type=pl.DeviceIdType.MESH,
            ).start()

    others = pl.ds(0, count - 1)
    loads[0].wait()
    loads[1].wait()
    group = width // split_x
    conducts = jnp.concatenate(
        [
            jnp.concatenate([ref[row][:, h * group : (h + 1) * group] for ref in (kx_ref, ky_ref)], 1)
            for row in range(rows)
            for h in range(split_x)
        ],
        0,
    )
    sent_k[...] = conducts.T.reshape(sent_k.shape)
    pl.semaphore_wait(barrier, count - 1)
    send_all(lambda at: sent_k.at[:, at], lambda at: got_k.at[:, at], k_sems)

    for load in loads[2:]:
        load.wait()
    field_of = lax.broadcasted_iota(jnp.int32, (span, width), 1) // levels
    scaled = [sigma_ref[row] * chi_ref[row] for row in range(rows)]
    stacked = jnp.dot(
        jnp.concatenate(
            [jnp.where(field_of == f, scaled[row], 0.0) for row in range(rows) for f in range(fields)],
            0,
        ),
        vertical_ref[...].reshape(width, levels),
        precision=lax.Precision.HIGHEST,
        preferred_element_type=jnp.float32,
    )
    sent_f[...] = stacked.T.reshape(sent_f.shape)
    send_all(lambda at: sent_f.at[at], lambda at: got_f.at[at], f_sems)
    got_k[:, me] = sent_k[:, me]
    got_f[me] = sent_f[me]

    lane = lax.broadcasted_iota(jnp.int32, (tall, LANES), 1)
    tile_row = lax.broadcasted_iota(jnp.int32, (tall, LANES), 0)
    cell_x = lane % length_x

    def tiles_on(values, tiles_by):
        moved = (tiles_by % split_y) * SUBLANES
        if moved == 0:
            return values
        return jnp.concatenate([values[-moved:], values[:-moved]], 0)

    def at_x(values, offset):
        return pltpu.roll(values, (LANES - offset) % LANES, 1)

    def at_y(values, offset):
        if abs(offset) >= rows:
            return tiles_on(values, -offset // rows)
        lanes = offset * length_x
        turned_by = pltpu.roll(values, (LANES - lanes) % LANES, 1)
        if offset < 0:
            return jnp.where(lane < -lanes, tiles_on(turned_by, 1), turned_by)
        return jnp.where(lane >= LANES - lanes, tiles_on(turned_by, -1), turned_by)

    pltpu.make_async_copy(got_k.at[:, others], got_k.at[:, others], k_sems.at[1]).wait()
    west = swap_blocks(got_k[0].reshape(tall, LANES), span, split_x)
    south = swap_blocks(got_k[1].reshape(tall, LANES), span, split_x)
    west = jnp.where(cell_x == 0, 0.0, west)
    south = jnp.where((tile_row < SUBLANES) & (lane < length_x), 0.0, south)
    x_operator = cyclic_reduction(west, length_x, at_x, lambda near: 3 * near < length_x)
    y_operator = cyclic_reduction(south, length_y, at_y, lambda near: 3 * near < rows)
    pltpu.make_async_copy(got_f.at[others], got_f.at[others], f_sems.at[1]).wait()
    field = swap_blocks(got_f[...].reshape(tall, LANES), span, split_x)
    for sweep in range(ITERS):
        field = reduced_solve(field, x_operator, at_x)
        field = reduced_solve(field, y_operator, at_y)
    solved[...] = swap_blocks(field, span, split_x).reshape(solved.shape)
    send_all(lambda at: solved.at[at], lambda at: back.at[at], back_sems)
    back[me] = solved[me]
    pltpu.make_async_copy(back.at[others], back.at[others], back_sems.at[1]).wait()
    turned = back[...].reshape(tall, LANES).T
    for row in range(rows):
        out_ref[row] = jnp.concatenate(
            [
                turned[(row * split_x + h) * span : (row * split_x + h + 1) * span]
                for h in range(split_x)
            ],
            1,
        )
    pltpu.make_async_copy(sent_k.at[:, others], sent_k.at[:, others], k_sems.at[0]).wait()
    pltpu.make_async_copy(sent_f.at[others], sent_f.at[others], f_sems.at[0]).wait()
    pltpu.make_async_copy(solved.at[others], solved.at[others], back_sems.at[0]).wait()


def channel_body(split_x, split_y, chi, sigma, vertical, kx, ky):
    count = split_x * split_y
    share = SUBLANES // split_x
    block = pltpu.VMEM(chi.shape, jnp.float32)
    packed = pltpu.VMEM((count, share, LANES), jnp.float32)
    packed_pair = pltpu.VMEM((2, count, share, LANES), jnp.float32)
    return pl.pallas_call(
        functools.partial(channel_kernel, split_x, split_y),
        out_shape=pltpu.VMEM(chi.shape, jnp.float32),
        in_specs=[pl.BlockSpec(memory_space=pl.ANY)] * 5,
        out_specs=pl.BlockSpec(memory_space=pltpu.VMEM),
        scratch_shapes=[
            block,
            block,
            pltpu.VMEM(vertical.shape, jnp.float32),
            block,
            block,
            packed_pair,
            packed_pair,
            packed,
            packed,
            packed,
            packed,
            pltpu.SemaphoreType.DMA((5,)),
            pltpu.SemaphoreType.DMA((2,)),
            pltpu.SemaphoreType.DMA((2,)),
            pltpu.SemaphoreType.DMA((2,)),
        ],
        compiler_params=pltpu.CompilerParams(collective_id=0, has_side_effects=True),
        name="channel_lines",
    )(chi, sigma, vertical, kx, ky)


def solution(mesh):
    split_x, split_y = (mesh.shape["gx"], mesh.shape["gy"])

    def chosen(chi, sigma, vertical, kx, ky):
        if channels_fit(chi.shape, vertical.shape[0], split_x, split_y):
            return channel_body(split_x, split_y, chi, sigma, vertical, kx, ky)
        return body(chi, sigma, vertical, kx, ky)


    placed = (
        P("gy", "gx", None),
        P("gy", "gx", None),
        P(),
        P("gy", "gx", None),
        P("gy", "gx", None),
    )
    return jax.shard_map(
        chosen, mesh=mesh, in_specs=placed, out_specs=P("gy", "gx", None), check_vma=False
    )
```

```python
import functools

import jax
import jax.numpy as jnp
from jax import lax
from jax.experimental import pallas as pl
from jax.experimental.pallas import tpu as pltpu
from jax.sharding import PartitionSpec as P

ITERS = 3


def mobius_join(earlier, later):
    top_left = later[0] * earlier[0] + later[1] * earlier[2]
    top_right = later[0] * earlier[1] + later[1] * earlier[3]
    low_left = later[2] * earlier[0] + later[3] * earlier[2]
    low_right = later[2] * earlier[1] + later[3] * earlier[3]
    factor = 1.0 / (top_left + top_right + low_left + low_right)
    return (top_left * factor, top_right * factor, low_left * factor, low_right * factor)


def affine_join(earlier, later):
    return (earlier[0] * later[0], later[0] * earlier[1] + later[1])


def mobius_value(matrix):
    return (matrix[0] + matrix[1]) / (matrix[2] + matrix[3])


def neutral(sample):
    filled = jnp.ones_like(sample[0])
    emptied = jnp.zeros_like(sample[0])
    if len(sample) == 4:
        return (filled, emptied, emptied, filled)
    return (filled, emptied)


def settle(gathered, split, join, position):
    ups = tuple((gathered[:, member_id] for member_id in range(split)))
    downs = tuple((gathered[:, member_id] for member_id in range(split, gathered.shape[1])))
    up_scan = lax.associative_scan(join, ups, axis=0)
    down_scan = lax.associative_scan(join, downs, reverse=True, axis=0)
    up_open = neutral(tuple((member[0] for member in ups)))
    down_open = neutral(tuple((member[0] for member in downs)))
    up_in = tuple(
        (
            lax.dynamic_index_in_dim(jnp.concatenate([anchor[None], member], 0), position, 0, False)
            for anchor, member in zip(up_open, up_scan)
        )
    )
    down_in = tuple(
        (
            lax.dynamic_index_in_dim(
                jnp.concatenate([member, anchor[None]], 0), position + 1, 0, False
            )
            for anchor, member in zip(down_open, down_scan)
        )
    )
    return (up_in, down_in)


def across_x(up_total, down_total, join):
    packed = jnp.stack(up_total + down_total, 0)[None]
    gathered = lax.all_gather(packed, "gx", axis=0, tiled=True)
    return settle(gathered, len(up_total), join, lax.axis_index("gx"))


def across_y(up_total, down_total, join):
    up_in = neutral(up_total)
    down_in = neutral(down_total)
    return (up_in, down_in)


def chain(up_elements, down_elements, join, axis_dim, across):
    span = up_elements[0].shape[axis_dim]
    up_local = lax.associative_scan(join, up_elements, axis=axis_dim)
    down_local = lax.associative_scan(join, down_elements, reverse=True, axis=axis_dim)
    up_total = tuple((lax.index_in_dim(member, span - 1, axis_dim, False) for member in up_local))
    down_total = tuple((lax.index_in_dim(member, 0, axis_dim, False) for member in down_local))
    up_in, down_in = across(up_total, down_total, join)
    up_whole = join(tuple((jnp.expand_dims(member, axis_dim) for member in up_in)), up_local)
    down_whole = join(tuple((jnp.expand_dims(member, axis_dim) for member in down_in)), down_local)
    return (up_in, up_whole, down_in, down_whole)


def open_edge(conduct, axis_dim, position):
    span = conduct.shape[axis_dim]
    place = lax.broadcasted_iota(jnp.int32, conduct.shape, axis_dim) + position * span
    return jnp.where(place == 0, jnp.zeros_like(conduct), conduct)


def operator_terms(kleft, axis_dim, across):
    span = kleft.shape[axis_dim]
    matrices = (1.0 + kleft, kleft, jnp.ones_like(kleft), kleft)
    up_in, up_whole, down_in, down_whole = chain(matrices, matrices, mobius_join, axis_dim, across)
    after = mobius_value(up_whole)
    before = jnp.concatenate(
        [
            jnp.expand_dims(mobius_value(up_in), axis_dim),
            lax.slice_in_dim(after, 0, span - 1, 1, axis_dim),
        ],
        axis_dim,
    )
    behind_whole = mobius_value(down_whole)
    behind = jnp.concatenate(
        [
            lax.slice_in_dim(behind_whole, 1, span, 1, axis_dim),
            jnp.expand_dims(mobius_value(down_in), axis_dim),
        ],
        axis_dim,
    )
    return (kleft / (before + kleft), kleft / (behind + kleft), after + behind - 1.0)


def line_solve(values, terms, axis_dim, across):
    forward_rate, backward_rate, diagonal = terms
    span = values.shape[axis_dim]
    up_in, up_whole, down_in, down_whole = chain(
        (forward_rate, values),
        (backward_rate, backward_rate * values),
        affine_join,
        axis_dim,
        across,
    )
    passed = down_whole[1]
    passed_next = jnp.concatenate(
        [lax.slice_in_dim(passed, 1, span, 1, axis_dim), jnp.expand_dims(down_in[1], axis_dim)],
        axis_dim,
    )
    return (up_whole[1] + passed_next) / diagonal


def to_lines(field, partners):
    row_count = field.shape[0]
    flattened = field.reshape(row_count, -1)
    padding = -flattened.shape[1] % partners
    return jnp.pad(flattened, ((0, 0), (0, padding)))


def from_lines(lines, target_shape):
    return lines[:, : target_shape[1] * target_shape[2]].reshape(target_shape)


def body(chi, sigma, vertical, kx, ky):
    fields = vertical.shape[0]
    levels = vertical.shape[1]
    width = fields * levels
    scaled = sigma * chi
    blocks = (
        jnp.eye(fields, dtype=jnp.float32)[:, None, :, None] * vertical[:, :, None, :]
    ).reshape(width, width)
    mixed = jnp.dot(scaled.reshape(-1, width), blocks, precision=lax.Precision.HIGHEST).reshape(
        scaled.shape
    )
    x_terms = operator_terms(open_edge(kx, 1, lax.axis_index("gx")), 1, across_x)
    partners = lax.axis_size("gy")
    whole_conduct = lax.all_to_all(
        to_lines(ky, partners), "gy", split_axis=1, concat_axis=0, tiled=True
    )
    y_terms = operator_terms(open_edge(whole_conduct, 0, 0), 0, across_y)
    current = mixed
    for sweep in range(ITERS):
        current = line_solve(current, x_terms, 1, across_x)
        whole_lines = lax.all_to_all(
            to_lines(current, partners), "gy", split_axis=1, concat_axis=0, tiled=True
        )
        solved = line_solve(whole_lines, y_terms, 0, across_y)
        current = from_lines(
            lax.all_to_all(solved, "gy", split_axis=0, concat_axis=1, tiled=True), current.shape
        )
    return current


LANES = 128
SUBLANES = 8


def channels_fit(shape, fields, split_x, split_y):
    rows, span, width = shape
    return (
        span == SUBLANES
        and rows * span * split_x == LANES
        and fields == split_x
        and SUBLANES % split_x == 0
        and width == SUBLANES * split_x * split_y
        and rows & (rows - 1) == 0
        and split_x & (split_x - 1) == 0
        and split_y & (split_y - 1) == 0
    )


def cyclic_reduction(kleft, length, at, paired):
    excess = jnp.ones_like(kleft)
    west = kleft
    east = at(kleft, 1)
    levels = []
    stride = 1
    while stride < length:
        inverse = 1.0 / (excess + west + east)
        from_west = west * at(inverse, -stride)
        from_east = east * at(inverse, stride)
        excess = excess + from_west * at(excess, -stride) + from_east * at(excess, stride)
        west = from_west * at(west, -stride)
        east = from_east * at(east, stride)
        levels.append((stride, from_west, from_east))
        stride *= 2
    steps = []
    while levels:
        near, west_near, east_near = levels.pop(0)
        if levels and paired(near):
            far, west_far, east_far = levels.pop(0)
            steps.append(
                (
                    (-near, west_near + west_far * at(east_near, -far)),
                    (near, east_near + east_far * at(west_near, far)),
                    (-far, west_far),
                    (far, east_far),
                    (-near - far, west_far * at(west_near, -far)),
                    (near + far, east_far * at(east_near, far)),
                )
            )
        else:
            steps.append(((-near, west_near), (near, east_near)))
    return steps, 1.0 / excess


def reduced_solve(values, operator, at):
    steps, inverse = operator
    for taps in steps:
        terms = [coefficient * at(values, offset) for offset, coefficient in taps]
        terms = [first + second for first, second in zip(terms[::2], terms[1::2])]
        values = (values + terms[0]) + sum(terms[2:], terms[1]) if terms[1:] else values + terms[0]
    return values * inverse


def swap_blocks(values, span, split_x):
    row = lax.broadcasted_iota(jnp.int32, values.shape, 0)
    lane = lax.broadcasted_iota(jnp.int32, values.shape, 1)
    down, along = (SUBLANES // split_x, span)
    while down < SUBLANES:
        row_bit = (row // down) % 2
        lane_bit = (lane // along) % 2
        later = pltpu.roll(pltpu.roll(values, along, 1), values.shape[0] - down, 0)
        earlier = pltpu.roll(pltpu.roll(values, LANES - along, 1), down, 0)
        values = jnp.where(row_bit == lane_bit, values, jnp.where(lane_bit == 1, later, earlier))
        down, along = (down * 2, along * 2)
    return values


def channel_kernel(
    split_x,
    split_y,
    chi_hbm,
    sigma_hbm,
    vertical_hbm,
    kx_hbm,
    ky_hbm,
    out_ref,
    chi_ref,
    sigma_ref,
    vertical_ref,
    kx_ref,
    ky_ref,
    sent,
    got,
    solved,
    back,
    load_sems,
    sems,
    back_sems,
):
    rows, span, width = chi_ref.shape
    fields, levels, _ = vertical_ref.shape
    count = split_x * split_y
    length_x = split_x * span
    length_y = split_y * rows
    tall = split_y * SUBLANES
    gx, gy = (lax.axis_index("gx"), lax.axis_index("gy"))
    me = gy * split_x + gx

    loads = [
        pltpu.make_async_copy(source, target, load_sems.at[number])
        for number, (source, target) in enumerate(
            (
                (kx_hbm, kx_ref),
                (ky_hbm, ky_ref),
                (chi_hbm, chi_ref),
                (sigma_hbm, sigma_ref),
                (vertical_hbm, vertical_ref),
            )
        )
    ]
    for load in loads:
        load.start()

    partners_x = [lax.bitwise_xor(gx, jnp.int32(step)) for step in range(split_x)]
    partners_y = [lax.bitwise_xor(gy, jnp.int32(step)) for step in range(split_y)]
    partners = [
        (partners_x[step_x], partners_y[step_y])
        for step_y in reversed(range(split_y))
        for step_x in range(split_x)
        if step_x or step_y
    ]

    barrier = pltpu.get_barrier_semaphore()
    for peer_x, peer_y in partners:
        pl.semaphore_signal(
            barrier,
            inc=1,
            device_id={"gx": peer_x, "gy": peer_y},
            device_id_type=pl.DeviceIdType.MESH,
        )

    def send_all(source, target, sems):
        for peer_x, peer_y in partners:
            pltpu.make_async_remote_copy(
                src_ref=source(peer_y * split_x + peer_x),
                dst_ref=target(me),
                send_sem=sems.at[0],
                recv_sem=sems.at[1],
                device_id={"gx": peer_x, "gy": peer_y},
                device_id_type=pl.DeviceIdType.MESH,
            ).start()

    others = pl.ds(0, count - 1)
    loads[0].wait()
    loads[1].wait()
    group = width // split_x
    conducts = jnp.concatenate(
        [
            jnp.concatenate([ref[row][:, h * group : (h + 1) * group] for ref in (kx_ref, ky_ref)], 1)
            for row in range(rows)
            for h in range(split_x)
        ],
        0,
    )
    conducts = conducts.T.reshape((2,) + back.shape)
    sent[:, 0] = conducts[0]
    sent[:, 1] = conducts[1]

    for load in loads[2:]:
        load.wait()
    field_of = lax.broadcasted_iota(jnp.int32, (span, width), 1) // levels
    scaled = [sigma_ref[row] * chi_ref[row] for row in range(rows)]
    stacked = jnp.dot(
        jnp.concatenate(
            [jnp.where(field_of == f, scaled[row], 0.0) for row in range(rows) for f in range(fields)],
            0,
        ),
        vertical_ref[...].reshape(width, levels),
        precision=lax.Precision.HIGHEST,
        preferred_element_type=jnp.float32,
    )
    sent[:, 2] = stacked.T.reshape(back.shape)
    pl.semaphore_wait(barrier, count - 1)
    send_all(lambda at: sent.at[at], lambda at: got.at[at], sems)
    got[me] = sent[me]

    lane = lax.broadcasted_iota(jnp.int32, (tall, LANES), 1)
    tile_row = lax.broadcasted_iota(jnp.int32, (tall, LANES), 0)
    cell_x = lane % length_x

    def tiles_on(values, tiles_by):
        moved = (tiles_by % split_y) * SUBLANES
        if moved == 0:
            return values
        return jnp.concatenate([values[-moved:], values[:-moved]], 0)

    def at_x(values, offset):
        return pltpu.roll(values, (LANES - offset) % LANES, 1)

    def at_y(values, offset):
        if abs(offset) >= rows:
            return tiles_on(values, -offset // rows)
        lanes = offset * length_x
        turned_by = pltpu.roll(values, (LANES - lanes) % LANES, 1)
        if offset < 0:
            return jnp.where(lane < -lanes, tiles_on(turned_by, 1), turned_by)
        return jnp.where(lane >= LANES - lanes, tiles_on(turned_by, -1), turned_by)

    pltpu.make_async_copy(got.at[others], got.at[others], sems.at[1]).wait()
    west = swap_blocks(got[:, 0].reshape(tall, LANES), span, split_x)
    south = swap_blocks(got[:, 1].reshape(tall, LANES), span, split_x)
    west = jnp.where(cell_x == 0, 0.0, west)
    south = jnp.where((tile_row < SUBLANES) & (lane < length_x), 0.0, south)
    x_operator = cyclic_reduction(west, length_x, at_x, lambda near: 3 * near < length_x)
    y_operator = cyclic_reduction(south, length_y, at_y, lambda near: 3 * near < rows)
    field = swap_blocks(got[:, 2].reshape(tall, LANES), span, split_x)
    for sweep in range(ITERS):
        field = reduced_solve(field, x_operator, at_x)
        field = reduced_solve(field, y_operator, at_y)
    solved[...] = swap_blocks(field, span, split_x).reshape(solved.shape)
    send_all(lambda at: solved.at[at], lambda at: back.at[at], back_sems)
    back[me] = solved[me]
    pltpu.make_async_copy(back.at[others], back.at[others], back_sems.at[1]).wait()
    turned = back[...].reshape(tall, LANES).T
    for row in range(rows):
        out_ref[row] = jnp.concatenate(
            [
                turned[(row * split_x + h) * span : (row * split_x + h + 1) * span]
                for h in range(split_x)
            ],
            1,
        )
    pltpu.make_async_copy(sent.at[others], sent.at[others], sems.at[0]).wait()
    pltpu.make_async_copy(solved.at[others], solved.at[others], back_sems.at[0]).wait()


def channel_body(split_x, split_y, chi, sigma, vertical, kx, ky):
    count = split_x * split_y
    share = SUBLANES // split_x
    block = pltpu.VMEM(chi.shape, jnp.float32)
    packed = pltpu.VMEM((count, share, LANES), jnp.float32)
    packed_triple = pltpu.VMEM((count, 3, share, LANES), jnp.float32)
    return pl.pallas_call(
        functools.partial(channel_kernel, split_x, split_y),
        out_shape=pltpu.VMEM(chi.shape, jnp.float32),
        in_specs=[pl.BlockSpec(memory_space=pl.ANY)] * 5,
        out_specs=pl.BlockSpec(memory_space=pltpu.VMEM),
        scratch_shapes=[
            block,
            block,
            pltpu.VMEM(vertical.shape, jnp.float32),
            block,
            block,
            packed_triple,
            packed_triple,
            packed,
            packed,
            pltpu.SemaphoreType.DMA((5,)),
            pltpu.SemaphoreType.DMA((2,)),
            pltpu.SemaphoreType.DMA((2,)),
        ],
        compiler_params=pltpu.CompilerParams(collective_id=0, has_side_effects=True),
        name="channel_lines",
    )(chi, sigma, vertical, kx, ky)


def solution(mesh):
    split_x, split_y = (mesh.shape["gx"], mesh.shape["gy"])

    def chosen(chi, sigma, vertical, kx, ky):
        if channels_fit(chi.shape, vertical.shape[0], split_x, split_y):
            return channel_body(split_x, split_y, chi, sigma, vertical, kx, ky)
        return body(chi, sigma, vertical, kx, ky)


    placed = (
        P("gy", "gx", None),
        P("gy", "gx", None),
        P(),
        P("gy", "gx", None),
        P("gy", "gx", None),
    )
    return jax.shard_map(
        chosen, mesh=mesh, in_specs=placed, out_specs=P("gy", "gx", None), check_vma=False
    )
```

```python
import functools

import jax
import jax.numpy as jnp
from jax import lax
from jax.experimental import pallas as pl
from jax.experimental.pallas import tpu as pltpu
from jax.sharding import PartitionSpec as P

ITERS = 3


def mobius_join(earlier, later):
    top_left = later[0] * earlier[0] + later[1] * earlier[2]
    top_right = later[0] * earlier[1] + later[1] * earlier[3]
    low_left = later[2] * earlier[0] + later[3] * earlier[2]
    low_right = later[2] * earlier[1] + later[3] * earlier[3]
    factor = 1.0 / (top_left + top_right + low_left + low_right)
    return (top_left * factor, top_right * factor, low_left * factor, low_right * factor)


def affine_join(earlier, later):
    return (earlier[0] * later[0], later[0] * earlier[1] + later[1])


def mobius_value(matrix):
    return (matrix[0] + matrix[1]) / (matrix[2] + matrix[3])


def neutral(sample):
    filled = jnp.ones_like(sample[0])
    emptied = jnp.zeros_like(sample[0])
    if len(sample) == 4:
        return (filled, emptied, emptied, filled)
    return (filled, emptied)


def settle(gathered, split, join, position):
    ups = tuple((gathered[:, member_id] for member_id in range(split)))
    downs = tuple((gathered[:, member_id] for member_id in range(split, gathered.shape[1])))
    up_scan = lax.associative_scan(join, ups, axis=0)
    down_scan = lax.associative_scan(join, downs, reverse=True, axis=0)
    up_open = neutral(tuple((member[0] for member in ups)))
    down_open = neutral(tuple((member[0] for member in downs)))
    up_in = tuple(
        (
            lax.dynamic_index_in_dim(jnp.concatenate([anchor[None], member], 0), position, 0, False)
            for anchor, member in zip(up_open, up_scan)
        )
    )
    down_in = tuple(
        (
            lax.dynamic_index_in_dim(
                jnp.concatenate([member, anchor[None]], 0), position + 1, 0, False
            )
            for anchor, member in zip(down_open, down_scan)
        )
    )
    return (up_in, down_in)


def across_x(up_total, down_total, join):
    packed = jnp.stack(up_total + down_total, 0)[None]
    gathered = lax.all_gather(packed, "gx", axis=0, tiled=True)
    return settle(gathered, len(up_total), join, lax.axis_index("gx"))


def across_y(up_total, down_total, join):
    up_in = neutral(up_total)
    down_in = neutral(down_total)
    return (up_in, down_in)


def chain(up_elements, down_elements, join, axis_dim, across):
    span = up_elements[0].shape[axis_dim]
    up_local = lax.associative_scan(join, up_elements, axis=axis_dim)
    down_local = lax.associative_scan(join, down_elements, reverse=True, axis=axis_dim)
    up_total = tuple((lax.index_in_dim(member, span - 1, axis_dim, False) for member in up_local))
    down_total = tuple((lax.index_in_dim(member, 0, axis_dim, False) for member in down_local))
    up_in, down_in = across(up_total, down_total, join)
    up_whole = join(tuple((jnp.expand_dims(member, axis_dim) for member in up_in)), up_local)
    down_whole = join(tuple((jnp.expand_dims(member, axis_dim) for member in down_in)), down_local)
    return (up_in, up_whole, down_in, down_whole)


def open_edge(conduct, axis_dim, position):
    span = conduct.shape[axis_dim]
    place = lax.broadcasted_iota(jnp.int32, conduct.shape, axis_dim) + position * span
    return jnp.where(place == 0, jnp.zeros_like(conduct), conduct)


def operator_terms(kleft, axis_dim, across):
    span = kleft.shape[axis_dim]
    matrices = (1.0 + kleft, kleft, jnp.ones_like(kleft), kleft)
    up_in, up_whole, down_in, down_whole = chain(matrices, matrices, mobius_join, axis_dim, across)
    after = mobius_value(up_whole)
    before = jnp.concatenate(
        [
            jnp.expand_dims(mobius_value(up_in), axis_dim),
            lax.slice_in_dim(after, 0, span - 1, 1, axis_dim),
        ],
        axis_dim,
    )
    behind_whole = mobius_value(down_whole)
    behind = jnp.concatenate(
        [
            lax.slice_in_dim(behind_whole, 1, span, 1, axis_dim),
            jnp.expand_dims(mobius_value(down_in), axis_dim),
        ],
        axis_dim,
    )
    return (kleft / (before + kleft), kleft / (behind + kleft), after + behind - 1.0)


def line_solve(values, terms, axis_dim, across):
    forward_rate, backward_rate, diagonal = terms
    span = values.shape[axis_dim]
    up_in, up_whole, down_in, down_whole = chain(
        (forward_rate, values),
        (backward_rate, backward_rate * values),
        affine_join,
        axis_dim,
        across,
    )
    passed = down_whole[1]
    passed_next = jnp.concatenate(
        [lax.slice_in_dim(passed, 1, span, 1, axis_dim), jnp.expand_dims(down_in[1], axis_dim)],
        axis_dim,
    )
    return (up_whole[1] + passed_next) / diagonal


def to_lines(field, partners):
    row_count = field.shape[0]
    flattened = field.reshape(row_count, -1)
    padding = -flattened.shape[1] % partners
    return jnp.pad(flattened, ((0, 0), (0, padding)))


def from_lines(lines, target_shape):
    return lines[:, : target_shape[1] * target_shape[2]].reshape(target_shape)


def body(chi, sigma, vertical, kx, ky):
    fields = vertical.shape[0]
    levels = vertical.shape[1]
    width = fields * levels
    scaled = sigma * chi
    blocks = (
        jnp.eye(fields, dtype=jnp.float32)[:, None, :, None] * vertical[:, :, None, :]
    ).reshape(width, width)
    mixed = jnp.dot(scaled.reshape(-1, width), blocks, precision=lax.Precision.HIGHEST).reshape(
        scaled.shape
    )
    x_terms = operator_terms(open_edge(kx, 1, lax.axis_index("gx")), 1, across_x)
    partners = lax.axis_size("gy")
    whole_conduct = lax.all_to_all(
        to_lines(ky, partners), "gy", split_axis=1, concat_axis=0, tiled=True
    )
    y_terms = operator_terms(open_edge(whole_conduct, 0, 0), 0, across_y)
    current = mixed
    for sweep in range(ITERS):
        current = line_solve(current, x_terms, 1, across_x)
        whole_lines = lax.all_to_all(
            to_lines(current, partners), "gy", split_axis=1, concat_axis=0, tiled=True
        )
        solved = line_solve(whole_lines, y_terms, 0, across_y)
        current = from_lines(
            lax.all_to_all(solved, "gy", split_axis=0, concat_axis=1, tiled=True), current.shape
        )
    return current


LANES = 128
SUBLANES = 8


def channels_fit(shape, fields, split_x, split_y):
    rows, span, width = shape
    return (
        span == SUBLANES
        and rows * span * split_x == LANES
        and fields == split_x
        and SUBLANES % split_x == 0
        and width == SUBLANES * split_x * split_y
        and rows & (rows - 1) == 0
        and split_x & (split_x - 1) == 0
        and split_y & (split_y - 1) == 0
    )


def cyclic_reduction(kleft, length, at, paired):
    excess = jnp.ones_like(kleft)
    west = kleft
    east = at(kleft, 1)
    levels = []
    stride = 1
    while stride < length:
        inverse = 1.0 / (excess + west + east)
        from_west = west * at(inverse, -stride)
        from_east = east * at(inverse, stride)
        excess = excess + from_west * at(excess, -stride) + from_east * at(excess, stride)
        west = from_west * at(west, -stride)
        east = from_east * at(east, stride)
        levels.append((stride, from_west, from_east))
        stride *= 2
    steps = []
    while levels:
        near, west_near, east_near = levels.pop(0)
        if levels and paired(near):
            far, west_far, east_far = levels.pop(0)
            steps.append(
                (
                    (-near, west_near + west_far * at(east_near, -far)),
                    (near, east_near + east_far * at(west_near, far)),
                    (-far, west_far),
                    (far, east_far),
                    (-near - far, west_far * at(west_near, -far)),
                    (near + far, east_far * at(east_near, far)),
                )
            )
        else:
            steps.append(((-near, west_near), (near, east_near)))
    return steps, 1.0 / excess


def reduced_solve(values, operator, at):
    steps, inverse = operator
    for taps in steps:
        terms = [coefficient * at(values, offset) for offset, coefficient in taps]
        terms = [first + second for first, second in zip(terms[::2], terms[1::2])]
        values = (values + terms[0]) + sum(terms[2:], terms[1]) if terms[1:] else values + terms[0]
    return values * inverse


def swap_blocks(values, span, split_x):
    share = SUBLANES // split_x
    tiles = values.reshape(-1, SUBLANES, LANES)
    group = lax.broadcasted_iota(jnp.int32, tiles.shape, 1) // share
    block = (lax.broadcasted_iota(jnp.int32, tiles.shape, 2) // span) % split_x
    apart = (block - group + split_x) % split_x
    swapped = tiles
    for k in range(1, split_x):
        ahead = pltpu.roll(tiles, span * k, 2)
        wrapped = pltpu.roll(tiles, LANES - span * (split_x - k), 2)
        moved = pltpu.roll(jnp.where(block >= k, ahead, wrapped), SUBLANES - share * k, 1)
        swapped = jnp.where(apart == k, moved, swapped)
    return swapped.reshape(values.shape)


def channel_kernel(
    split_x,
    split_y,
    chi_hbm,
    sigma_hbm,
    vertical_hbm,
    kx_hbm,
    ky_hbm,
    out_ref,
    chi_ref,
    sigma_ref,
    vertical_ref,
    kx_ref,
    ky_ref,
    sent,
    got,
    solved,
    back,
    load_sems,
    sems,
    back_sems,
):
    rows, span, width = chi_ref.shape
    fields, levels, _ = vertical_ref.shape
    count = split_x * split_y
    length_x = split_x * span
    length_y = split_y * rows
    tall = split_y * SUBLANES
    gx, gy = (lax.axis_index("gx"), lax.axis_index("gy"))
    me = gy * split_x + gx

    loads = [
        pltpu.make_async_copy(source, target, load_sems.at[number])
        for number, (source, target) in enumerate(
            (
                (kx_hbm, kx_ref),
                (ky_hbm, ky_ref),
                (chi_hbm, chi_ref),
                (sigma_hbm, sigma_ref),
                (vertical_hbm, vertical_ref),
            )
        )
    ]
    for load in loads:
        load.start()

    partners_x = [lax.bitwise_xor(gx, jnp.int32(step)) for step in range(split_x)]
    partners_y = [lax.bitwise_xor(gy, jnp.int32(step)) for step in range(split_y)]
    partners = [
        (partners_x[step_x], partners_y[step_y])
        for step_y in reversed(range(split_y))
        for step_x in range(split_x)
        if step_x or step_y
    ]

    barrier = pltpu.get_barrier_semaphore()
    for peer_x, peer_y in partners:
        pl.semaphore_signal(
            barrier,
            inc=1,
            device_id={"gx": peer_x, "gy": peer_y},
            device_id_type=pl.DeviceIdType.MESH,
        )

    def send_all(source, target, sems):
        for peer_x, peer_y in partners:
            pltpu.make_async_remote_copy(
                src_ref=source(peer_y * split_x + peer_x),
                dst_ref=target(me),
                send_sem=sems.at[0],
                recv_sem=sems.at[1],
                device_id={"gx": peer_x, "gy": peer_y},
                device_id_type=pl.DeviceIdType.MESH,
            ).start()

    others = pl.ds(0, count - 1)
    loads[0].wait()
    loads[1].wait()
    group = width // split_x
    conducts = jnp.concatenate(
        [
            jnp.concatenate([ref[row][:, h * group : (h + 1) * group] for ref in (kx_ref, ky_ref)], 1)
            for row in range(rows)
            for h in range(split_x)
        ],
        0,
    )
    conducts = conducts.T.reshape((2,) + back.shape)
    sent[:, 0] = conducts[0]
    sent[:, 1] = conducts[1]

    for load in loads[2:]:
        load.wait()
    field_of = lax.broadcasted_iota(jnp.int32, (span, width), 1) // levels
    scaled = [sigma_ref[row] * chi_ref[row] for row in range(rows)]
    stacked = jnp.dot(
        jnp.concatenate(
            [jnp.where(field_of == f, scaled[row], 0.0) for row in range(rows) for f in range(fields)],
            0,
        ),
        vertical_ref[...].reshape(width, levels),
        precision=lax.Precision.HIGHEST,
        preferred_element_type=jnp.float32,
    )
    sent[:, 2] = stacked.T.reshape(back.shape)
    pl.semaphore_wait(barrier, count - 1)
    send_all(lambda at: sent.at[at], lambda at: got.at[at], sems)
    got[me] = sent[me]

    lane = lax.broadcasted_iota(jnp.int32, (tall, LANES), 1)
    tile_row = lax.broadcasted_iota(jnp.int32, (tall, LANES), 0)
    cell_x = lane % length_x

    def tiles_on(values, tiles_by):
        moved = (tiles_by % split_y) * SUBLANES
        if moved == 0:
            return values
        return jnp.concatenate([values[-moved:], values[:-moved]], 0)

    def at_x(values, offset):
        return pltpu.roll(values, (LANES - offset) % LANES, 1)

    def at_y(values, offset):
        if abs(offset) >= rows:
            return tiles_on(values, -offset // rows)
        lanes = offset * length_x
        turned_by = pltpu.roll(values, (LANES - lanes) % LANES, 1)
        if offset < 0:
            return jnp.where(lane < -lanes, tiles_on(turned_by, 1), turned_by)
        return jnp.where(lane >= LANES - lanes, tiles_on(turned_by, -1), turned_by)

    pltpu.make_async_copy(got.at[others], got.at[others], sems.at[1]).wait()
    west = swap_blocks(got[:, 0].reshape(tall, LANES), span, split_x)
    south = swap_blocks(got[:, 1].reshape(tall, LANES), span, split_x)
    west = jnp.where(cell_x == 0, 0.0, west)
    south = jnp.where((tile_row < SUBLANES) & (lane < length_x), 0.0, south)
    x_operator = cyclic_reduction(west, length_x, at_x, lambda near: 3 * near < length_x)
    y_operator = cyclic_reduction(south, length_y, at_y, lambda near: 3 * near < rows)
    field = swap_blocks(got[:, 2].reshape(tall, LANES), span, split_x)
    for sweep in range(ITERS):
        field = reduced_solve(field, x_operator, at_x)
        field = reduced_solve(field, y_operator, at_y)
    solved[...] = swap_blocks(field, span, split_x).reshape(solved.shape)
    send_all(lambda at: solved.at[at], lambda at: back.at[at], back_sems)
    back[me] = solved[me]
    pltpu.make_async_copy(back.at[others], back.at[others], back_sems.at[1]).wait()
    turned = back[...].reshape(tall, LANES).T
    for row in range(rows):
        out_ref[row] = jnp.concatenate(
            [
                turned[(row * split_x + h) * span : (row * split_x + h + 1) * span]
                for h in range(split_x)
            ],
            1,
        )
    pltpu.make_async_copy(sent.at[others], sent.at[others], sems.at[0]).wait()
    pltpu.make_async_copy(solved.at[others], solved.at[others], back_sems.at[0]).wait()


def channel_body(split_x, split_y, chi, sigma, vertical, kx, ky):
    count = split_x * split_y
    share = SUBLANES // split_x
    block = pltpu.VMEM(chi.shape, jnp.float32)
    packed = pltpu.VMEM((count, share, LANES), jnp.float32)
    packed_triple = pltpu.VMEM((count, 3, share, LANES), jnp.float32)
    return pl.pallas_call(
        functools.partial(channel_kernel, split_x, split_y),
        out_shape=pltpu.VMEM(chi.shape, jnp.float32),
        in_specs=[pl.BlockSpec(memory_space=pl.ANY)] * 5,
        out_specs=pl.BlockSpec(memory_space=pltpu.VMEM),
        scratch_shapes=[
            block,
            block,
            pltpu.VMEM(vertical.shape, jnp.float32),
            block,
            block,
            packed_triple,
            packed_triple,
            packed,
            packed,
            pltpu.SemaphoreType.DMA((5,)),
            pltpu.SemaphoreType.DMA((2,)),
            pltpu.SemaphoreType.DMA((2,)),
        ],
        compiler_params=pltpu.CompilerParams(collective_id=0, has_side_effects=True),
        name="channel_lines",
    )(chi, sigma, vertical, kx, ky)


def solution(mesh):
    split_x, split_y = (mesh.shape["gx"], mesh.shape["gy"])

    def chosen(chi, sigma, vertical, kx, ky):
        if channels_fit(chi.shape, vertical.shape[0], split_x, split_y):
            return channel_body(split_x, split_y, chi, sigma, vertical, kx, ky)
        return body(chi, sigma, vertical, kx, ky)


    placed = (
        P("gy", "gx", None),
        P("gy", "gx", None),
        P(),
        P("gy", "gx", None),
        P("gy", "gx", None),
    )
    return jax.shard_map(
        chosen, mesh=mesh, in_specs=placed, out_specs=P("gy", "gx", None), check_vma=False
    )
```

```python
import functools

import jax
import jax.numpy as jnp
from jax import lax
from jax.experimental import pallas as pl
from jax.experimental.pallas import tpu as pltpu
from jax.sharding import PartitionSpec as P

ITERS = 3


def mobius_join(earlier, later):
    top_left = later[0] * earlier[0] + later[1] * earlier[2]
    top_right = later[0] * earlier[1] + later[1] * earlier[3]
    low_left = later[2] * earlier[0] + later[3] * earlier[2]
    low_right = later[2] * earlier[1] + later[3] * earlier[3]
    factor = 1.0 / (top_left + top_right + low_left + low_right)
    return (top_left * factor, top_right * factor, low_left * factor, low_right * factor)


def affine_join(earlier, later):
    return (earlier[0] * later[0], later[0] * earlier[1] + later[1])


def mobius_value(matrix):
    return (matrix[0] + matrix[1]) / (matrix[2] + matrix[3])


def neutral(sample):
    filled = jnp.ones_like(sample[0])
    emptied = jnp.zeros_like(sample[0])
    if len(sample) == 4:
        return (filled, emptied, emptied, filled)
    return (filled, emptied)


def settle(gathered, split, join, position):
    ups = tuple((gathered[:, member_id] for member_id in range(split)))
    downs = tuple((gathered[:, member_id] for member_id in range(split, gathered.shape[1])))
    up_scan = lax.associative_scan(join, ups, axis=0)
    down_scan = lax.associative_scan(join, downs, reverse=True, axis=0)
    up_open = neutral(tuple((member[0] for member in ups)))
    down_open = neutral(tuple((member[0] for member in downs)))
    up_in = tuple(
        (
            lax.dynamic_index_in_dim(jnp.concatenate([anchor[None], member], 0), position, 0, False)
            for anchor, member in zip(up_open, up_scan)
        )
    )
    down_in = tuple(
        (
            lax.dynamic_index_in_dim(
                jnp.concatenate([member, anchor[None]], 0), position + 1, 0, False
            )
            for anchor, member in zip(down_open, down_scan)
        )
    )
    return (up_in, down_in)


def across_x(up_total, down_total, join):
    packed = jnp.stack(up_total + down_total, 0)[None]
    gathered = lax.all_gather(packed, "gx", axis=0, tiled=True)
    return settle(gathered, len(up_total), join, lax.axis_index("gx"))


def across_y(up_total, down_total, join):
    up_in = neutral(up_total)
    down_in = neutral(down_total)
    return (up_in, down_in)


def chain(up_elements, down_elements, join, axis_dim, across):
    span = up_elements[0].shape[axis_dim]
    up_local = lax.associative_scan(join, up_elements, axis=axis_dim)
    down_local = lax.associative_scan(join, down_elements, reverse=True, axis=axis_dim)
    up_total = tuple((lax.index_in_dim(member, span - 1, axis_dim, False) for member in up_local))
    down_total = tuple((lax.index_in_dim(member, 0, axis_dim, False) for member in down_local))
    up_in, down_in = across(up_total, down_total, join)
    up_whole = join(tuple((jnp.expand_dims(member, axis_dim) for member in up_in)), up_local)
    down_whole = join(tuple((jnp.expand_dims(member, axis_dim) for member in down_in)), down_local)
    return (up_in, up_whole, down_in, down_whole)


def open_edge(conduct, axis_dim, position):
    span = conduct.shape[axis_dim]
    place = lax.broadcasted_iota(jnp.int32, conduct.shape, axis_dim) + position * span
    return jnp.where(place == 0, jnp.zeros_like(conduct), conduct)


def operator_terms(kleft, axis_dim, across):
    span = kleft.shape[axis_dim]
    matrices = (1.0 + kleft, kleft, jnp.ones_like(kleft), kleft)
    up_in, up_whole, down_in, down_whole = chain(matrices, matrices, mobius_join, axis_dim, across)
    after = mobius_value(up_whole)
    before = jnp.concatenate(
        [
            jnp.expand_dims(mobius_value(up_in), axis_dim),
            lax.slice_in_dim(after, 0, span - 1, 1, axis_dim),
        ],
        axis_dim,
    )
    behind_whole = mobius_value(down_whole)
    behind = jnp.concatenate(
        [
            lax.slice_in_dim(behind_whole, 1, span, 1, axis_dim),
            jnp.expand_dims(mobius_value(down_in), axis_dim),
        ],
        axis_dim,
    )
    return (kleft / (before + kleft), kleft / (behind + kleft), after + behind - 1.0)


def line_solve(values, terms, axis_dim, across):
    forward_rate, backward_rate, diagonal = terms
    span = values.shape[axis_dim]
    up_in, up_whole, down_in, down_whole = chain(
        (forward_rate, values),
        (backward_rate, backward_rate * values),
        affine_join,
        axis_dim,
        across,
    )
    passed = down_whole[1]
    passed_next = jnp.concatenate(
        [lax.slice_in_dim(passed, 1, span, 1, axis_dim), jnp.expand_dims(down_in[1], axis_dim)],
        axis_dim,
    )
    return (up_whole[1] + passed_next) / diagonal


def to_lines(field, partners):
    row_count = field.shape[0]
    flattened = field.reshape(row_count, -1)
    padding = -flattened.shape[1] % partners
    return jnp.pad(flattened, ((0, 0), (0, padding)))


def from_lines(lines, target_shape):
    return lines[:, : target_shape[1] * target_shape[2]].reshape(target_shape)


def body(chi, sigma, vertical, kx, ky):
    fields = vertical.shape[0]
    levels = vertical.shape[1]
    width = fields * levels
    scaled = sigma * chi
    blocks = (
        jnp.eye(fields, dtype=jnp.float32)[:, None, :, None] * vertical[:, :, None, :]
    ).reshape(width, width)
    mixed = jnp.dot(scaled.reshape(-1, width), blocks, precision=lax.Precision.HIGHEST).reshape(
        scaled.shape
    )
    x_terms = operator_terms(open_edge(kx, 1, lax.axis_index("gx")), 1, across_x)
    partners = lax.axis_size("gy")
    whole_conduct = lax.all_to_all(
        to_lines(ky, partners), "gy", split_axis=1, concat_axis=0, tiled=True
    )
    y_terms = operator_terms(open_edge(whole_conduct, 0, 0), 0, across_y)
    current = mixed
    for sweep in range(ITERS):
        current = line_solve(current, x_terms, 1, across_x)
        whole_lines = lax.all_to_all(
            to_lines(current, partners), "gy", split_axis=1, concat_axis=0, tiled=True
        )
        solved = line_solve(whole_lines, y_terms, 0, across_y)
        current = from_lines(
            lax.all_to_all(solved, "gy", split_axis=0, concat_axis=1, tiled=True), current.shape
        )
    return current


LANES = 128
SUBLANES = 8


def channels_fit(shape, fields, split_x, split_y):
    rows, span, width = shape
    return (
        span == SUBLANES
        and rows * span * split_x == LANES
        and fields == split_x
        and SUBLANES % split_x == 0
        and width == SUBLANES * split_x * split_y
        and rows & (rows - 1) == 0
        and split_x & (split_x - 1) == 0
        and split_y & (split_y - 1) == 0
    )


def cyclic_reduction(kleft, length, at, paired):
    excess = jnp.ones_like(kleft)
    west = kleft
    east = at(kleft, 1)
    levels = []
    stride = 1
    while stride < length:
        inverse = 1.0 / (excess + west + east)
        from_west = west * at(inverse, -stride)
        from_east = east * at(inverse, stride)
        excess = excess + from_west * at(excess, -stride) + from_east * at(excess, stride)
        west = from_west * at(west, -stride)
        east = from_east * at(east, stride)
        levels.append((stride, from_west, from_east))
        stride *= 2
    steps = []
    while levels:
        near, west_near, east_near = levels.pop(0)
        if levels and paired(near):
            far, west_far, east_far = levels.pop(0)
            steps.append(
                (
                    (-near, west_near + west_far * at(east_near, -far)),
                    (near, east_near + east_far * at(west_near, far)),
                    (-far, west_far),
                    (far, east_far),
                    (-near - far, west_far * at(west_near, -far)),
                    (near + far, east_far * at(east_near, far)),
                )
            )
        else:
            steps.append(((-near, west_near), (near, east_near)))
    return steps, 1.0 / excess


def reduced_solve(values, operator, at):
    steps, inverse = operator
    for taps in steps:
        terms = [coefficient * at(values, offset) for offset, coefficient in taps]
        terms = [first + second for first, second in zip(terms[::2], terms[1::2])]
        values = (values + terms[0]) + sum(terms[2:], terms[1]) if terms[1:] else values + terms[0]
    return values * inverse


def swap_blocks(values, span, split_x):
    share = SUBLANES // split_x
    tiles = values.reshape(-1, SUBLANES, LANES)
    group = lax.broadcasted_iota(jnp.int32, tiles.shape, 1) // share
    block = (lax.broadcasted_iota(jnp.int32, tiles.shape, 2) // span) % split_x
    apart = (block - group + split_x) % split_x
    swapped = tiles
    for k in range(1, split_x):
        ahead = pltpu.roll(tiles, span * k, 2)
        wrapped = pltpu.roll(tiles, LANES - span * (split_x - k), 2)
        moved = pltpu.roll(jnp.where(block >= k, ahead, wrapped), SUBLANES - share * k, 1)
        swapped = jnp.where(apart == k, moved, swapped)
    return swapped.reshape(values.shape)


def channel_kernel(
    split_x,
    split_y,
    chi_hbm,
    sigma_hbm,
    vertical_hbm,
    kx_hbm,
    ky_hbm,
    out_ref,
    chi_ref,
    sigma_ref,
    vertical_ref,
    kx_ref,
    ky_ref,
    sent,
    got,
    solved,
    back,
    load_sems,
    sems,
    back_sems,
):
    rows, span, width = chi_ref.shape
    fields, levels, _ = vertical_ref.shape
    count = split_x * split_y
    length_x = split_x * span
    length_y = split_y * rows
    tall = split_y * SUBLANES
    gx, gy = (lax.axis_index("gx"), lax.axis_index("gy"))
    me = gy * split_x + gx

    loads = [
        pltpu.make_async_copy(source, target, load_sems.at[number])
        for number, (source, target) in enumerate(
            (
                (kx_hbm, kx_ref),
                (ky_hbm, ky_ref),
                (chi_hbm, chi_ref),
                (sigma_hbm, sigma_ref),
                (vertical_hbm, vertical_ref),
            )
        )
    ]
    for load in loads:
        load.start()

    partners_x = [lax.bitwise_xor(gx, jnp.int32(step)) for step in reversed(range(split_x))]

    def each_partner(act):
        def line(number, _):
            peer_y = lax.bitwise_xor(gy, split_y - 1 - number)
            for peer_x in partners_x:
                act(peer_x, peer_y)
            return 0

        lax.fori_loop(0, split_y - 1, line, 0)
        for peer_x in partners_x[:-1]:
            act(peer_x, gy)

    barrier = pltpu.get_barrier_semaphore()

    def greet(peer_x, peer_y):
        pl.semaphore_signal(
            barrier,
            inc=1,
            device_id={"gx": peer_x, "gy": peer_y},
            device_id_type=pl.DeviceIdType.MESH,
        )

    each_partner(greet)

    def send_all(source, target, sems):
        def send(peer_x, peer_y):
            pltpu.make_async_remote_copy(
                src_ref=source(peer_y * split_x + peer_x),
                dst_ref=target(me),
                send_sem=sems.at[0],
                recv_sem=sems.at[1],
                device_id={"gx": peer_x, "gy": peer_y},
                device_id_type=pl.DeviceIdType.MESH,
            ).start()

        each_partner(send)

    others = pl.ds(0, count - 1)
    loads[0].wait()
    loads[1].wait()
    group = width // split_x
    conducts = jnp.concatenate(
        [
            jnp.concatenate([ref[row][:, h * group : (h + 1) * group] for ref in (kx_ref, ky_ref)], 1)
            for row in range(rows)
            for h in range(split_x)
        ],
        0,
    )
    conducts = conducts.T.reshape((2,) + back.shape)
    sent[:, 0] = conducts[0]
    sent[:, 1] = conducts[1]

    for load in loads[2:]:
        load.wait()
    field_of = lax.broadcasted_iota(jnp.int32, (span, width), 1) // levels
    scaled = [sigma_ref[row] * chi_ref[row] for row in range(rows)]
    stacked = jnp.dot(
        jnp.concatenate(
            [jnp.where(field_of == f, scaled[row], 0.0) for row in range(rows) for f in range(fields)],
            0,
        ),
        vertical_ref[...].reshape(width, levels),
        precision=lax.Precision.HIGHEST,
        preferred_element_type=jnp.float32,
    )
    sent[:, 2] = stacked.T.reshape(back.shape)
    pl.semaphore_wait(barrier, count - 1)
    send_all(lambda at: sent.at[at], lambda at: got.at[at], sems)
    got[me] = sent[me]

    lane = lax.broadcasted_iota(jnp.int32, (tall, LANES), 1)
    tile_row = lax.broadcasted_iota(jnp.int32, (tall, LANES), 0)
    cell_x = lane % length_x

    def tiles_on(values, tiles_by):
        moved = (tiles_by % split_y) * SUBLANES
        if moved == 0:
            return values
        return jnp.concatenate([values[-moved:], values[:-moved]], 0)

    def at_x(values, offset):
        return pltpu.roll(values, (LANES - offset) % LANES, 1)

    def at_y(values, offset):
        if abs(offset) >= rows:
            return tiles_on(values, -offset // rows)
        lanes = offset * length_x
        turned_by = pltpu.roll(values, (LANES - lanes) % LANES, 1)
        if offset < 0:
            return jnp.where(lane < -lanes, tiles_on(turned_by, 1), turned_by)
        return jnp.where(lane >= LANES - lanes, tiles_on(turned_by, -1), turned_by)

    pltpu.make_async_copy(got.at[others], got.at[others], sems.at[1]).wait()
    west = swap_blocks(got[:, 0].reshape(tall, LANES), span, split_x)
    south = swap_blocks(got[:, 1].reshape(tall, LANES), span, split_x)
    west = jnp.where(cell_x == 0, 0.0, west)
    south = jnp.where((tile_row < SUBLANES) & (lane < length_x), 0.0, south)
    x_operator = cyclic_reduction(west, length_x, at_x, lambda near: 3 * near < length_x)
    y_operator = cyclic_reduction(south, length_y, at_y, lambda near: 3 * near < rows)
    field = swap_blocks(got[:, 2].reshape(tall, LANES), span, split_x)

    def sweep(number, field):
        field = reduced_solve(field, x_operator, at_x)
        return reduced_solve(field, y_operator, at_y)

    field = lax.fori_loop(0, ITERS, sweep, field)
    solved[...] = swap_blocks(field, span, split_x).reshape(solved.shape)
    send_all(lambda at: solved.at[at], lambda at: back.at[at], back_sems)
    back[me] = solved[me]
    pltpu.make_async_copy(back.at[others], back.at[others], back_sems.at[1]).wait()
    turned = back[...].reshape(tall, LANES).T
    for row in range(rows):
        out_ref[row] = jnp.concatenate(
            [
                turned[(row * split_x + h) * span : (row * split_x + h + 1) * span]
                for h in range(split_x)
            ],
            1,
        )
    pltpu.make_async_copy(sent.at[others], sent.at[others], sems.at[0]).wait()
    pltpu.make_async_copy(solved.at[others], solved.at[others], back_sems.at[0]).wait()


def channel_body(split_x, split_y, chi, sigma, vertical, kx, ky):
    count = split_x * split_y
    share = SUBLANES // split_x
    block = pltpu.VMEM(chi.shape, jnp.float32)
    packed = pltpu.VMEM((count, share, LANES), jnp.float32)
    packed_triple = pltpu.VMEM((count, 3, share, LANES), jnp.float32)
    return pl.pallas_call(
        functools.partial(channel_kernel, split_x, split_y),
        out_shape=pltpu.VMEM(chi.shape, jnp.float32),
        in_specs=[pl.BlockSpec(memory_space=pl.ANY)] * 5,
        out_specs=pl.BlockSpec(memory_space=pltpu.VMEM),
        scratch_shapes=[
            block,
            block,
            pltpu.VMEM(vertical.shape, jnp.float32),
            block,
            block,
            packed_triple,
            packed_triple,
            packed,
            packed,
            pltpu.SemaphoreType.DMA((5,)),
            pltpu.SemaphoreType.DMA((2,)),
            pltpu.SemaphoreType.DMA((2,)),
        ],
        compiler_params=pltpu.CompilerParams(collective_id=0, has_side_effects=True),
        name="channel_lines",
    )(chi, sigma, vertical, kx, ky)


def solution(mesh):
    split_x, split_y = (mesh.shape["gx"], mesh.shape["gy"])

    def chosen(chi, sigma, vertical, kx, ky):
        if channels_fit(chi.shape, vertical.shape[0], split_x, split_y):
            return channel_body(split_x, split_y, chi, sigma, vertical, kx, ky)
        return body(chi, sigma, vertical, kx, ky)


    placed = (
        P("gy", "gx", None),
        P("gy", "gx", None),
        P(),
        P("gy", "gx", None),
        P("gy", "gx", None),
    )
    return jax.shard_map(
        chosen, mesh=mesh, in_specs=placed, out_specs=P("gy", "gx", None), check_vma=False
    )
```

```python
import functools

import jax
import jax.numpy as jnp
from jax import lax
from jax.experimental import pallas as pl
from jax.experimental.pallas import tpu as pltpu
from jax.sharding import PartitionSpec as P

ITERS = 3


def mobius_join(earlier, later):
    top_left = later[0] * earlier[0] + later[1] * earlier[2]
    top_right = later[0] * earlier[1] + later[1] * earlier[3]
    low_left = later[2] * earlier[0] + later[3] * earlier[2]
    low_right = later[2] * earlier[1] + later[3] * earlier[3]
    factor = 1.0 / (top_left + top_right + low_left + low_right)
    return (top_left * factor, top_right * factor, low_left * factor, low_right * factor)


def affine_join(earlier, later):
    return (earlier[0] * later[0], later[0] * earlier[1] + later[1])


def mobius_value(matrix):
    return (matrix[0] + matrix[1]) / (matrix[2] + matrix[3])


def neutral(sample):
    filled = jnp.ones_like(sample[0])
    emptied = jnp.zeros_like(sample[0])
    if len(sample) == 4:
        return (filled, emptied, emptied, filled)
    return (filled, emptied)


def settle(gathered, split, join, position):
    ups = tuple((gathered[:, member_id] for member_id in range(split)))
    downs = tuple((gathered[:, member_id] for member_id in range(split, gathered.shape[1])))
    up_scan = lax.associative_scan(join, ups, axis=0)
    down_scan = lax.associative_scan(join, downs, reverse=True, axis=0)
    up_open = neutral(tuple((member[0] for member in ups)))
    down_open = neutral(tuple((member[0] for member in downs)))
    up_in = tuple(
        (
            lax.dynamic_index_in_dim(jnp.concatenate([anchor[None], member], 0), position, 0, False)
            for anchor, member in zip(up_open, up_scan)
        )
    )
    down_in = tuple(
        (
            lax.dynamic_index_in_dim(
                jnp.concatenate([member, anchor[None]], 0), position + 1, 0, False
            )
            for anchor, member in zip(down_open, down_scan)
        )
    )
    return (up_in, down_in)


def across_x(up_total, down_total, join):
    packed = jnp.stack(up_total + down_total, 0)[None]
    gathered = lax.all_gather(packed, "gx", axis=0, tiled=True)
    return settle(gathered, len(up_total), join, lax.axis_index("gx"))


def across_y(up_total, down_total, join):
    up_in = neutral(up_total)
    down_in = neutral(down_total)
    return (up_in, down_in)


def chain(up_elements, down_elements, join, axis_dim, across):
    span = up_elements[0].shape[axis_dim]
    up_local = lax.associative_scan(join, up_elements, axis=axis_dim)
    down_local = lax.associative_scan(join, down_elements, reverse=True, axis=axis_dim)
    up_total = tuple((lax.index_in_dim(member, span - 1, axis_dim, False) for member in up_local))
    down_total = tuple((lax.index_in_dim(member, 0, axis_dim, False) for member in down_local))
    up_in, down_in = across(up_total, down_total, join)
    up_whole = join(tuple((jnp.expand_dims(member, axis_dim) for member in up_in)), up_local)
    down_whole = join(tuple((jnp.expand_dims(member, axis_dim) for member in down_in)), down_local)
    return (up_in, up_whole, down_in, down_whole)


def open_edge(conduct, axis_dim, position):
    span = conduct.shape[axis_dim]
    place = lax.broadcasted_iota(jnp.int32, conduct.shape, axis_dim) + position * span
    return jnp.where(place == 0, jnp.zeros_like(conduct), conduct)


def operator_terms(kleft, axis_dim, across):
    span = kleft.shape[axis_dim]
    matrices = (1.0 + kleft, kleft, jnp.ones_like(kleft), kleft)
    up_in, up_whole, down_in, down_whole = chain(matrices, matrices, mobius_join, axis_dim, across)
    after = mobius_value(up_whole)
    before = jnp.concatenate(
        [
            jnp.expand_dims(mobius_value(up_in), axis_dim),
            lax.slice_in_dim(after, 0, span - 1, 1, axis_dim),
        ],
        axis_dim,
    )
    behind_whole = mobius_value(down_whole)
    behind = jnp.concatenate(
        [
            lax.slice_in_dim(behind_whole, 1, span, 1, axis_dim),
            jnp.expand_dims(mobius_value(down_in), axis_dim),
        ],
        axis_dim,
    )
    return (kleft / (before + kleft), kleft / (behind + kleft), after + behind - 1.0)


def line_solve(values, terms, axis_dim, across):
    forward_rate, backward_rate, diagonal = terms
    span = values.shape[axis_dim]
    up_in, up_whole, down_in, down_whole = chain(
        (forward_rate, values),
        (backward_rate, backward_rate * values),
        affine_join,
        axis_dim,
        across,
    )
    passed = down_whole[1]
    passed_next = jnp.concatenate(
        [lax.slice_in_dim(passed, 1, span, 1, axis_dim), jnp.expand_dims(down_in[1], axis_dim)],
        axis_dim,
    )
    return (up_whole[1] + passed_next) / diagonal


def to_lines(field, partners):
    row_count = field.shape[0]
    flattened = field.reshape(row_count, -1)
    padding = -flattened.shape[1] % partners
    return jnp.pad(flattened, ((0, 0), (0, padding)))


def from_lines(lines, target_shape):
    return lines[:, : target_shape[1] * target_shape[2]].reshape(target_shape)


def body(chi, sigma, vertical, kx, ky):
    fields = vertical.shape[0]
    levels = vertical.shape[1]
    width = fields * levels
    scaled = sigma * chi
    blocks = (
        jnp.eye(fields, dtype=jnp.float32)[:, None, :, None] * vertical[:, :, None, :]
    ).reshape(width, width)
    mixed = jnp.dot(scaled.reshape(-1, width), blocks, precision=lax.Precision.HIGHEST).reshape(
        scaled.shape
    )
    x_terms = operator_terms(open_edge(kx, 1, lax.axis_index("gx")), 1, across_x)
    partners = lax.axis_size("gy")
    whole_conduct = lax.all_to_all(
        to_lines(ky, partners), "gy", split_axis=1, concat_axis=0, tiled=True
    )
    y_terms = operator_terms(open_edge(whole_conduct, 0, 0), 0, across_y)
    current = mixed
    for sweep in range(ITERS):
        current = line_solve(current, x_terms, 1, across_x)
        whole_lines = lax.all_to_all(
            to_lines(current, partners), "gy", split_axis=1, concat_axis=0, tiled=True
        )
        solved = line_solve(whole_lines, y_terms, 0, across_y)
        current = from_lines(
            lax.all_to_all(solved, "gy", split_axis=0, concat_axis=1, tiled=True), current.shape
        )
    return current


LANES = 128
SUBLANES = 8


def channels_fit(shape, fields, split_x, split_y):
    rows, span, width = shape
    return (
        span == SUBLANES
        and rows * span * split_x == LANES
        and fields == split_x
        and SUBLANES % split_x == 0
        and width == SUBLANES * split_x * split_y
        and rows & (rows - 1) == 0
        and split_x & (split_x - 1) == 0
        and split_y & (split_y - 1) == 0
    )


def cyclic_reduction(kleft, length, at, paired):
    excess = jnp.ones_like(kleft)
    west = kleft
    east = at(kleft, 1)
    levels = []
    stride = 1
    while stride < length:
        inverse = 1.0 / (excess + west + east)
        from_west = west * at(inverse, -stride)
        from_east = east * at(inverse, stride)
        excess = excess + from_west * at(excess, -stride) + from_east * at(excess, stride)
        west = from_west * at(west, -stride)
        east = from_east * at(east, stride)
        levels.append((stride, from_west, from_east))
        stride *= 2
    steps = []
    while levels:
        near, west_near, east_near = levels.pop(0)
        if levels and paired(near):
            far, west_far, east_far = levels.pop(0)
            steps.append(
                (
                    (-near, west_near + west_far * at(east_near, -far)),
                    (near, east_near + east_far * at(west_near, far)),
                    (-far, west_far),
                    (far, east_far),
                    (-near - far, west_far * at(west_near, -far)),
                    (near + far, east_far * at(east_near, far)),
                )
            )
        else:
            steps.append(((-near, west_near), (near, east_near)))
    return steps, 1.0 / excess


def reduced_solve(values, operator, at):
    steps, inverse = operator
    for taps in steps:
        terms = [coefficient * at(values, offset) for offset, coefficient in taps]
        terms = [first + second for first, second in zip(terms[::2], terms[1::2])]
        values = (values + terms[0]) + sum(terms[2:], terms[1]) if terms[1:] else values + terms[0]
    return values * inverse


def swap_blocks(values, span, split_x):
    share = SUBLANES // split_x
    tiles = values.reshape(-1, SUBLANES, LANES)
    group = lax.broadcasted_iota(jnp.int32, tiles.shape, 1) // share
    block = (lax.broadcasted_iota(jnp.int32, tiles.shape, 2) // span) % split_x
    apart = (block - group + split_x) % split_x
    swapped = tiles
    for k in range(1, split_x):
        ahead = pltpu.roll(tiles, span * k, 2)
        wrapped = pltpu.roll(tiles, LANES - span * (split_x - k), 2)
        moved = pltpu.roll(jnp.where(block >= k, ahead, wrapped), SUBLANES - share * k, 1)
        swapped = jnp.where(apart == k, moved, swapped)
    return swapped.reshape(values.shape)


def channel_kernel(
    split_x,
    split_y,
    chi_hbm,
    sigma_hbm,
    vertical_hbm,
    kx_hbm,
    ky_hbm,
    out_ref,
    chi_ref,
    sigma_ref,
    vertical_ref,
    kx_ref,
    ky_ref,
    sent_flat,
    got_flat,
    solved_flat,
    back_flat,
    load_sems,
    sems,
    back_sems,
):
    rows, span, width = chi_ref.shape
    fields, levels, _ = vertical_ref.shape
    count = split_x * split_y
    length_x = split_x * span
    length_y = split_y * rows
    tall = split_y * SUBLANES
    pieces = (count, SUBLANES // split_x, LANES)
    sent, got = (flat.reshape((3,) + pieces) for flat in (sent_flat, got_flat))
    solved, back = (flat.reshape(pieces) for flat in (solved_flat, back_flat))
    gx, gy = (lax.axis_index("gx"), lax.axis_index("gy"))
    me = gy * split_x + gx

    loads = [
        pltpu.make_async_copy(source, target, load_sems.at[number])
        for number, (source, target) in enumerate(
            (
                (kx_hbm, kx_ref),
                (ky_hbm, ky_ref),
                (chi_hbm, chi_ref),
                (sigma_hbm, sigma_ref),
                (vertical_hbm, vertical_ref),
            )
        )
    ]
    for load in loads:
        load.start()

    partners_x = [lax.bitwise_xor(gx, jnp.int32(step)) for step in range(split_x)]
    partners_y = [lax.bitwise_xor(gy, jnp.int32(step)) for step in range(split_y)]
    partners = [
        (partners_x[step_x], partners_y[step_y])
        for step_y in reversed(range(split_y))
        for step_x in range(split_x)
        if step_x or step_y
    ]

    barrier = pltpu.get_barrier_semaphore()
    for peer_x, peer_y in partners:
        pl.semaphore_signal(
            barrier,
            inc=1,
            device_id={"gx": peer_x, "gy": peer_y},
            device_id_type=pl.DeviceIdType.MESH,
        )

    def send_all(source, target, sems):
        for peer_x, peer_y in partners:
            pltpu.make_async_remote_copy(
                src_ref=source(peer_y * split_x + peer_x),
                dst_ref=target(me),
                send_sem=sems.at[0],
                recv_sem=sems.at[1],
                device_id={"gx": peer_x, "gy": peer_y},
                device_id_type=pl.DeviceIdType.MESH,
            ).start()

    others = pl.ds(0, count - 1)
    loads[0].wait()
    loads[1].wait()
    group = width // split_x
    conducts = jnp.concatenate(
        [
            jnp.concatenate([ref[row][:, h * group : (h + 1) * group] for ref in (kx_ref, ky_ref)], 1)
            for row in range(rows)
            for h in range(split_x)
        ],
        0,
    )
    sent_flat[: 2 * tall] = conducts.T

    for load in loads[2:]:
        load.wait()
    field_of = lax.broadcasted_iota(jnp.int32, (span, width), 1) // levels
    scaled = [sigma_ref[row] * chi_ref[row] for row in range(rows)]
    stacked = jnp.dot(
        jnp.concatenate(
            [jnp.where(field_of == f, scaled[row], 0.0) for row in range(rows) for f in range(fields)],
            0,
        ),
        vertical_ref[...].reshape(width, levels),
        precision=lax.Precision.HIGHEST,
        preferred_element_type=jnp.float32,
    )
    sent_flat[2 * tall :] = stacked.T
    pl.semaphore_wait(barrier, count - 1)
    send_all(lambda at: sent.at[:, at], lambda at: got.at[:, at], sems)
    mine = pltpu.make_async_copy(sent.at[:, me], got.at[:, me], load_sems.at[0])
    mine.start()

    lane = lax.broadcasted_iota(jnp.int32, (tall, LANES), 1)
    tile_row = lax.broadcasted_iota(jnp.int32, (tall, LANES), 0)
    cell_x = lane % length_x

    def tiles_on(values, tiles_by):
        moved = (tiles_by % split_y) * SUBLANES
        if moved == 0:
            return values
        return jnp.concatenate([values[-moved:], values[:-moved]], 0)

    def at_x(values, offset):
        return pltpu.roll(values, (LANES - offset) % LANES, 1)

    def at_y(values, offset):
        if abs(offset) >= rows:
            return tiles_on(values, -offset // rows)
        lanes = offset * length_x
        turned_by = pltpu.roll(values, (LANES - lanes) % LANES, 1)
        if offset < 0:
            return jnp.where(lane < -lanes, tiles_on(turned_by, 1), turned_by)
        return jnp.where(lane >= LANES - lanes, tiles_on(turned_by, -1), turned_by)

    pltpu.make_async_copy(got.at[:, others], got.at[:, others], sems.at[1]).wait()
    mine.wait()
    west = swap_blocks(got_flat[0 * tall : 1 * tall], span, split_x)
    south = swap_blocks(got_flat[1 * tall : 2 * tall], span, split_x)
    west = jnp.where(cell_x == 0, 0.0, west)
    south = jnp.where((tile_row < SUBLANES) & (lane < length_x), 0.0, south)
    x_operator = cyclic_reduction(west, length_x, at_x, lambda near: 3 * near < length_x)
    y_operator = cyclic_reduction(south, length_y, at_y, lambda near: 3 * near < rows)
    field = swap_blocks(got_flat[2 * tall : 3 * tall], span, split_x)
    for sweep in range(ITERS):
        field = reduced_solve(field, x_operator, at_x)
        field = reduced_solve(field, y_operator, at_y)
    solved_flat[...] = swap_blocks(field, span, split_x)
    send_all(lambda at: solved.at[at], lambda at: back.at[at], back_sems)
    mine = pltpu.make_async_copy(solved.at[me], back.at[me], load_sems.at[0])
    mine.start()
    pltpu.make_async_copy(back.at[others], back.at[others], back_sems.at[1]).wait()
    mine.wait()
    turned = back_flat[...].T
    for row in range(rows):
        out_ref[row] = jnp.concatenate(
            [
                turned[(row * split_x + h) * span : (row * split_x + h + 1) * span]
                for h in range(split_x)
            ],
            1,
        )
    pltpu.make_async_copy(sent.at[:, others], sent.at[:, others], sems.at[0]).wait()
    pltpu.make_async_copy(solved.at[others], solved.at[others], back_sems.at[0]).wait()


def channel_body(split_x, split_y, chi, sigma, vertical, kx, ky):
    tall = split_y * SUBLANES
    block = pltpu.VMEM(chi.shape, jnp.float32)
    packed = pltpu.VMEM((tall, LANES), jnp.float32)
    packed_triple = pltpu.VMEM((3 * tall, LANES), jnp.float32)
    return pl.pallas_call(
        functools.partial(channel_kernel, split_x, split_y),
        out_shape=pltpu.VMEM(chi.shape, jnp.float32),
        in_specs=[pl.BlockSpec(memory_space=pl.ANY)] * 5,
        out_specs=pl.BlockSpec(memory_space=pltpu.VMEM),
        scratch_shapes=[
            block,
            block,
            pltpu.VMEM(vertical.shape, jnp.float32),
            block,
            block,
            packed_triple,
            packed_triple,
            packed,
            packed,
            pltpu.SemaphoreType.DMA((5,)),
            pltpu.SemaphoreType.DMA((2,)),
            pltpu.SemaphoreType.DMA((2,)),
        ],
        compiler_params=pltpu.CompilerParams(collective_id=0, has_side_effects=True),
        name="channel_lines",
    )(chi, sigma, vertical, kx, ky)


def solution(mesh):
    split_x, split_y = (mesh.shape["gx"], mesh.shape["gy"])

    def chosen(chi, sigma, vertical, kx, ky):
        if channels_fit(chi.shape, vertical.shape[0], split_x, split_y):
            return channel_body(split_x, split_y, chi, sigma, vertical, kx, ky)
        return body(chi, sigma, vertical, kx, ky)


    placed = (
        P("gy", "gx", None),
        P("gy", "gx", None),
        P(),
        P("gy", "gx", None),
        P("gy", "gx", None),
    )
    return jax.shard_map(
        chosen, mesh=mesh, in_specs=placed, out_specs=P("gy", "gx", None), check_vma=False
    )
```

```python
import functools

import jax
import jax.numpy as jnp
from jax import lax
from jax.experimental import pallas as pl
from jax.experimental.pallas import tpu as pltpu
from jax.sharding import PartitionSpec as P

ITERS = 3


def mobius_join(earlier, later):
    top_left = later[0] * earlier[0] + later[1] * earlier[2]
    top_right = later[0] * earlier[1] + later[1] * earlier[3]
    low_left = later[2] * earlier[0] + later[3] * earlier[2]
    low_right = later[2] * earlier[1] + later[3] * earlier[3]
    factor = 1.0 / (top_left + top_right + low_left + low_right)
    return (top_left * factor, top_right * factor, low_left * factor, low_right * factor)


def affine_join(earlier, later):
    return (earlier[0] * later[0], later[0] * earlier[1] + later[1])


def mobius_value(matrix):
    return (matrix[0] + matrix[1]) / (matrix[2] + matrix[3])


def neutral(sample):
    filled = jnp.ones_like(sample[0])
    emptied = jnp.zeros_like(sample[0])
    if len(sample) == 4:
        return (filled, emptied, emptied, filled)
    return (filled, emptied)


def settle(gathered, split, join, position):
    ups = tuple((gathered[:, member_id] for member_id in range(split)))
    downs = tuple((gathered[:, member_id] for member_id in range(split, gathered.shape[1])))
    up_scan = lax.associative_scan(join, ups, axis=0)
    down_scan = lax.associative_scan(join, downs, reverse=True, axis=0)
    up_open = neutral(tuple((member[0] for member in ups)))
    down_open = neutral(tuple((member[0] for member in downs)))
    up_in = tuple(
        (
            lax.dynamic_index_in_dim(jnp.concatenate([anchor[None], member], 0), position, 0, False)
            for anchor, member in zip(up_open, up_scan)
        )
    )
    down_in = tuple(
        (
            lax.dynamic_index_in_dim(
                jnp.concatenate([member, anchor[None]], 0), position + 1, 0, False
            )
            for anchor, member in zip(down_open, down_scan)
        )
    )
    return (up_in, down_in)


def across_x(up_total, down_total, join):
    packed = jnp.stack(up_total + down_total, 0)[None]
    gathered = lax.all_gather(packed, "gx", axis=0, tiled=True)
    return settle(gathered, len(up_total), join, lax.axis_index("gx"))


def across_y(up_total, down_total, join):
    up_in = neutral(up_total)
    down_in = neutral(down_total)
    return (up_in, down_in)


def chain(up_elements, down_elements, join, axis_dim, across):
    span = up_elements[0].shape[axis_dim]
    up_local = lax.associative_scan(join, up_elements, axis=axis_dim)
    down_local = lax.associative_scan(join, down_elements, reverse=True, axis=axis_dim)
    up_total = tuple((lax.index_in_dim(member, span - 1, axis_dim, False) for member in up_local))
    down_total = tuple((lax.index_in_dim(member, 0, axis_dim, False) for member in down_local))
    up_in, down_in = across(up_total, down_total, join)
    up_whole = join(tuple((jnp.expand_dims(member, axis_dim) for member in up_in)), up_local)
    down_whole = join(tuple((jnp.expand_dims(member, axis_dim) for member in down_in)), down_local)
    return (up_in, up_whole, down_in, down_whole)


def open_edge(conduct, axis_dim, position):
    span = conduct.shape[axis_dim]
    place = lax.broadcasted_iota(jnp.int32, conduct.shape, axis_dim) + position * span
    return jnp.where(place == 0, jnp.zeros_like(conduct), conduct)


def operator_terms(kleft, axis_dim, across):
    span = kleft.shape[axis_dim]
    matrices = (1.0 + kleft, kleft, jnp.ones_like(kleft), kleft)
    up_in, up_whole, down_in, down_whole = chain(matrices, matrices, mobius_join, axis_dim, across)
    after = mobius_value(up_whole)
    before = jnp.concatenate(
        [
            jnp.expand_dims(mobius_value(up_in), axis_dim),
            lax.slice_in_dim(after, 0, span - 1, 1, axis_dim),
        ],
        axis_dim,
    )
    behind_whole = mobius_value(down_whole)
    behind = jnp.concatenate(
        [
            lax.slice_in_dim(behind_whole, 1, span, 1, axis_dim),
            jnp.expand_dims(mobius_value(down_in), axis_dim),
        ],
        axis_dim,
    )
    return (kleft / (before + kleft), kleft / (behind + kleft), after + behind - 1.0)


def line_solve(values, terms, axis_dim, across):
    forward_rate, backward_rate, diagonal = terms
    span = values.shape[axis_dim]
    up_in, up_whole, down_in, down_whole = chain(
        (forward_rate, values),
        (backward_rate, backward_rate * values),
        affine_join,
        axis_dim,
        across,
    )
    passed = down_whole[1]
    passed_next = jnp.concatenate(
        [lax.slice_in_dim(passed, 1, span, 1, axis_dim), jnp.expand_dims(down_in[1], axis_dim)],
        axis_dim,
    )
    return (up_whole[1] + passed_next) / diagonal


def to_lines(field, partners):
    row_count = field.shape[0]
    flattened = field.reshape(row_count, -1)
    padding = -flattened.shape[1] % partners
    return jnp.pad(flattened, ((0, 0), (0, padding)))


def from_lines(lines, target_shape):
    return lines[:, : target_shape[1] * target_shape[2]].reshape(target_shape)


def body(chi, sigma, vertical, kx, ky):
    fields = vertical.shape[0]
    levels = vertical.shape[1]
    width = fields * levels
    scaled = sigma * chi
    blocks = (
        jnp.eye(fields, dtype=jnp.float32)[:, None, :, None] * vertical[:, :, None, :]
    ).reshape(width, width)
    mixed = jnp.dot(scaled.reshape(-1, width), blocks, precision=lax.Precision.HIGHEST).reshape(
        scaled.shape
    )
    x_terms = operator_terms(open_edge(kx, 1, lax.axis_index("gx")), 1, across_x)
    partners = lax.axis_size("gy")
    whole_conduct = lax.all_to_all(
        to_lines(ky, partners), "gy", split_axis=1, concat_axis=0, tiled=True
    )
    y_terms = operator_terms(open_edge(whole_conduct, 0, 0), 0, across_y)
    current = mixed
    for sweep in range(ITERS):
        current = line_solve(current, x_terms, 1, across_x)
        whole_lines = lax.all_to_all(
            to_lines(current, partners), "gy", split_axis=1, concat_axis=0, tiled=True
        )
        solved = line_solve(whole_lines, y_terms, 0, across_y)
        current = from_lines(
            lax.all_to_all(solved, "gy", split_axis=0, concat_axis=1, tiled=True), current.shape
        )
    return current


LANES = 128
SUBLANES = 8


def channels_fit(shape, fields, split_x, split_y):
    rows, span, width = shape
    return (
        span == SUBLANES
        and rows * span * split_x == LANES
        and fields == split_x
        and SUBLANES % split_x == 0
        and width == SUBLANES * split_x * split_y
        and rows & (rows - 1) == 0
        and split_x & (split_x - 1) == 0
        and split_y & (split_y - 1) == 0
    )


def cyclic_reduction(kleft, length, at, paired, values):
    excess = jnp.ones_like(kleft)
    west = kleft
    east = at(kleft, 1)
    levels = []
    stride = 1
    while stride < length:
        inverse = 1.0 / (excess + west + east)
        from_west = west * at(inverse, -stride)
        from_east = east * at(inverse, stride)
        excess = excess + from_west * at(excess, -stride) + from_east * at(excess, stride)
        west = from_west * at(west, -stride)
        east = from_east * at(east, stride)
        levels.append((stride, from_west, from_east))
        if values is not None:
            values = values + (from_west * at(values, -stride) + from_east * at(values, stride))
        stride *= 2
    inverse = 1.0 / excess
    if values is not None:
        values = values * inverse
    steps = []
    while levels:
        near, west_near, east_near = levels.pop(0)
        if levels and paired(near):
            far, west_far, east_far = levels.pop(0)
            steps.append(
                (
                    (-near, west_near + west_far * at(east_near, -far)),
                    (near, east_near + east_far * at(west_near, far)),
                    (-far, west_far),
                    (far, east_far),
                    (-near - far, west_far * at(west_near, -far)),
                    (near + far, east_far * at(east_near, far)),
                )
            )
        else:
            steps.append(((-near, west_near), (near, east_near)))
    return (steps, inverse), values


def reduced_solve(values, operator, at):
    steps, inverse = operator
    for taps in steps:
        terms = [coefficient * at(values, offset) for offset, coefficient in taps]
        terms = [first + second for first, second in zip(terms[::2], terms[1::2])]
        values = (values + terms[0]) + sum(terms[2:], terms[1]) if terms[1:] else values + terms[0]
    return values * inverse


def swap_blocks(values, span, split_x):
    share = SUBLANES // split_x
    tiles = values.reshape(-1, SUBLANES, LANES)
    group = lax.broadcasted_iota(jnp.int32, tiles.shape, 1) // share
    block = (lax.broadcasted_iota(jnp.int32, tiles.shape, 2) // span) % split_x
    apart = (block - group + split_x) % split_x
    swapped = tiles
    for k in range(1, split_x):
        ahead = pltpu.roll(tiles, span * k, 2)
        wrapped = pltpu.roll(tiles, LANES - span * (split_x - k), 2)
        moved = pltpu.roll(jnp.where(block >= k, ahead, wrapped), SUBLANES - share * k, 1)
        swapped = jnp.where(apart == k, moved, swapped)
    return swapped.reshape(values.shape)


def channel_kernel(
    split_x,
    split_y,
    chi_hbm,
    sigma_hbm,
    vertical_hbm,
    kx_hbm,
    ky_hbm,
    out_ref,
    chi_ref,
    sigma_ref,
    vertical_ref,
    kx_ref,
    ky_ref,
    sent_flat,
    got_flat,
    solved_flat,
    back_flat,
    load_sems,
    sems,
    back_sems,
):
    rows, span, width = chi_ref.shape
    fields, levels, _ = vertical_ref.shape
    count = split_x * split_y
    length_x = split_x * span
    length_y = split_y * rows
    tall = split_y * SUBLANES
    pieces = (count, SUBLANES // split_x, LANES)
    sent, got = (flat.reshape((3,) + pieces) for flat in (sent_flat, got_flat))
    solved, back = (flat.reshape(pieces) for flat in (solved_flat, back_flat))
    gx, gy = (lax.axis_index("gx"), lax.axis_index("gy"))
    me = gy * split_x + gx

    loads = [
        pltpu.make_async_copy(source, target, load_sems.at[number])
        for number, (source, target) in enumerate(
            (
                (kx_hbm, kx_ref),
                (ky_hbm, ky_ref),
                (chi_hbm, chi_ref),
                (sigma_hbm, sigma_ref),
                (vertical_hbm, vertical_ref),
            )
        )
    ]
    for load in loads:
        load.start()

    partners_x = [lax.bitwise_xor(gx, jnp.int32(step)) for step in range(split_x)]
    partners_y = [lax.bitwise_xor(gy, jnp.int32(step)) for step in range(split_y)]
    partners = [
        (partners_x[step_x], partners_y[step_y])
        for step_y in reversed(range(split_y))
        for step_x in reversed(range(split_x))
        if step_x or step_y
    ]

    barrier = pltpu.get_barrier_semaphore()
    for peer_x, peer_y in partners:
        pl.semaphore_signal(
            barrier,
            inc=1,
            device_id={"gx": peer_x, "gy": peer_y},
            device_id_type=pl.DeviceIdType.MESH,
        )

    def send_all(source, target, sems):
        for peer_x, peer_y in partners:
            pltpu.make_async_remote_copy(
                src_ref=source(peer_y * split_x + peer_x),
                dst_ref=target(me),
                send_sem=sems.at[0],
                recv_sem=sems.at[1],
                device_id={"gx": peer_x, "gy": peer_y},
                device_id_type=pl.DeviceIdType.MESH,
            ).start()

    others = pl.ds(0, count - 1)
    loads[0].wait()
    loads[1].wait()
    group = width // split_x
    conducts = jnp.concatenate(
        [
            jnp.concatenate([ref[row][:, h * group : (h + 1) * group] for ref in (kx_ref, ky_ref)], 1)
            for row in range(rows)
            for h in range(split_x)
        ],
        0,
    )
    sent_flat[: 2 * tall] = conducts.T

    for load in loads[2:]:
        load.wait()
    field_of = lax.broadcasted_iota(jnp.int32, (span, width), 1) // levels
    scaled = [sigma_ref[row] * chi_ref[row] for row in range(rows)]
    stacked = jnp.dot(
        jnp.concatenate(
            [jnp.where(field_of == f, scaled[row], 0.0) for row in range(rows) for f in range(fields)],
            0,
        ),
        vertical_ref[...].reshape(width, levels),
        precision=lax.Precision.HIGHEST,
        preferred_element_type=jnp.float32,
    )
    sent_flat[2 * tall :] = stacked.T
    pl.semaphore_wait(barrier, count - 1)
    send_all(lambda at: sent.at[:, at], lambda at: got.at[:, at], sems)
    mine = pltpu.make_async_copy(sent.at[:, me], got.at[:, me], load_sems.at[0])
    mine.start()

    lane = lax.broadcasted_iota(jnp.int32, (tall, LANES), 1)
    tile_row = lax.broadcasted_iota(jnp.int32, (tall, LANES), 0)
    cell_x = lane % length_x

    def tiles_on(values, tiles_by):
        moved = (tiles_by % split_y) * SUBLANES
        if moved == 0:
            return values
        return jnp.concatenate([values[-moved:], values[:-moved]], 0)

    def at_x(values, offset):
        return pltpu.roll(values, (LANES - offset) % LANES, 1)

    def at_y(values, offset):
        if abs(offset) >= rows:
            return tiles_on(values, -offset // rows)
        lanes = offset * length_x
        turned_by = pltpu.roll(values, (LANES - lanes) % LANES, 1)
        if offset < 0:
            return jnp.where(lane < -lanes, tiles_on(turned_by, 1), turned_by)
        return jnp.where(lane >= LANES - lanes, tiles_on(turned_by, -1), turned_by)

    pltpu.make_async_copy(got.at[:, others], got.at[:, others], sems.at[1]).wait()
    mine.wait()
    west = swap_blocks(got_flat[0 * tall : 1 * tall], span, split_x)
    south = swap_blocks(got_flat[1 * tall : 2 * tall], span, split_x)
    west = jnp.where(cell_x == 0, 0.0, west)
    south = jnp.where((tile_row < SUBLANES) & (lane < length_x), 0.0, south)
    field = swap_blocks(got_flat[2 * tall : 3 * tall], span, split_x)
    x_operator, field = cyclic_reduction(
        west, length_x, at_x, lambda near: 3 * near < length_x, field
    )
    y_operator, _ = cyclic_reduction(south, length_y, at_y, lambda near: 3 * near < rows, None)
    for sweep in range(ITERS):
        if sweep:
            field = reduced_solve(field, x_operator, at_x)
        field = reduced_solve(field, y_operator, at_y)
    solved_flat[...] = swap_blocks(field, span, split_x)
    send_all(lambda at: solved.at[at], lambda at: back.at[at], back_sems)
    mine = pltpu.make_async_copy(solved.at[me], back.at[me], load_sems.at[0])
    mine.start()
    pltpu.make_async_copy(back.at[others], back.at[others], back_sems.at[1]).wait()
    mine.wait()
    turned = back_flat[...].T
    for row in range(rows):
        out_ref[row] = jnp.concatenate(
            [
                turned[(row * split_x + h) * span : (row * split_x + h + 1) * span]
                for h in range(split_x)
            ],
            1,
        )
    pltpu.make_async_copy(sent.at[:, others], sent.at[:, others], sems.at[0]).wait()
    pltpu.make_async_copy(solved.at[others], solved.at[others], back_sems.at[0]).wait()


def channel_body(split_x, split_y, chi, sigma, vertical, kx, ky):
    tall = split_y * SUBLANES
    block = pltpu.VMEM(chi.shape, jnp.float32)
    packed = pltpu.VMEM((tall, LANES), jnp.float32)
    packed_triple = pltpu.VMEM((3 * tall, LANES), jnp.float32)
    return pl.pallas_call(
        functools.partial(channel_kernel, split_x, split_y),
        out_shape=pltpu.VMEM(chi.shape, jnp.float32),
        in_specs=[pl.BlockSpec(memory_space=pl.ANY)] * 5,
        out_specs=pl.BlockSpec(memory_space=pltpu.VMEM),
        scratch_shapes=[
            block,
            block,
            pltpu.VMEM(vertical.shape, jnp.float32),
            block,
            block,
            packed_triple,
            packed_triple,
            packed,
            packed,
            pltpu.SemaphoreType.DMA((5,)),
            pltpu.SemaphoreType.DMA((2,)),
            pltpu.SemaphoreType.DMA((2,)),
        ],
        compiler_params=pltpu.CompilerParams(collective_id=0, has_side_effects=True),
        name="channel_lines",
    )(chi, sigma, vertical, kx, ky)


def solution(mesh):
    split_x, split_y = (mesh.shape["gx"], mesh.shape["gy"])

    def chosen(chi, sigma, vertical, kx, ky):
        if channels_fit(chi.shape, vertical.shape[0], split_x, split_y):
            return channel_body(split_x, split_y, chi, sigma, vertical, kx, ky)
        return body(chi, sigma, vertical, kx, ky)


    placed = (
        P("gy", "gx", None),
        P("gy", "gx", None),
        P(),
        P("gy", "gx", None),
        P("gy", "gx", None),
    )
    return jax.shard_map(
        chosen, mesh=mesh, in_specs=placed, out_specs=P("gy", "gx", None), check_vma=False
    )
```

```python
import functools

import jax
import jax.numpy as jnp
from jax import lax
from jax.experimental import pallas as pl
from jax.experimental.pallas import tpu as pltpu
from jax.sharding import PartitionSpec as P

ITERS = 3


def mobius_join(earlier, later):
    top_left = later[0] * earlier[0] + later[1] * earlier[2]
    top_right = later[0] * earlier[1] + later[1] * earlier[3]
    low_left = later[2] * earlier[0] + later[3] * earlier[2]
    low_right = later[2] * earlier[1] + later[3] * earlier[3]
    factor = 1.0 / (top_left + top_right + low_left + low_right)
    return (top_left * factor, top_right * factor, low_left * factor, low_right * factor)


def affine_join(earlier, later):
    return (earlier[0] * later[0], later[0] * earlier[1] + later[1])


def mobius_value(matrix):
    return (matrix[0] + matrix[1]) / (matrix[2] + matrix[3])


def neutral(sample):
    filled = jnp.ones_like(sample[0])
    emptied = jnp.zeros_like(sample[0])
    if len(sample) == 4:
        return (filled, emptied, emptied, filled)
    return (filled, emptied)


def settle(gathered, split, join, position):
    ups = tuple((gathered[:, member_id] for member_id in range(split)))
    downs = tuple((gathered[:, member_id] for member_id in range(split, gathered.shape[1])))
    up_scan = lax.associative_scan(join, ups, axis=0)
    down_scan = lax.associative_scan(join, downs, reverse=True, axis=0)
    up_open = neutral(tuple((member[0] for member in ups)))
    down_open = neutral(tuple((member[0] for member in downs)))
    up_in = tuple(
        (
            lax.dynamic_index_in_dim(jnp.concatenate([anchor[None], member], 0), position, 0, False)
            for anchor, member in zip(up_open, up_scan)
        )
    )
    down_in = tuple(
        (
            lax.dynamic_index_in_dim(
                jnp.concatenate([member, anchor[None]], 0), position + 1, 0, False
            )
            for anchor, member in zip(down_open, down_scan)
        )
    )
    return (up_in, down_in)


def across_x(up_total, down_total, join):
    packed = jnp.stack(up_total + down_total, 0)[None]
    gathered = lax.all_gather(packed, "gx", axis=0, tiled=True)
    return settle(gathered, len(up_total), join, lax.axis_index("gx"))


def across_y(up_total, down_total, join):
    up_in = neutral(up_total)
    down_in = neutral(down_total)
    return (up_in, down_in)


def chain(up_elements, down_elements, join, axis_dim, across):
    span = up_elements[0].shape[axis_dim]
    up_local = lax.associative_scan(join, up_elements, axis=axis_dim)
    down_local = lax.associative_scan(join, down_elements, reverse=True, axis=axis_dim)
    up_total = tuple((lax.index_in_dim(member, span - 1, axis_dim, False) for member in up_local))
    down_total = tuple((lax.index_in_dim(member, 0, axis_dim, False) for member in down_local))
    up_in, down_in = across(up_total, down_total, join)
    up_whole = join(tuple((jnp.expand_dims(member, axis_dim) for member in up_in)), up_local)
    down_whole = join(tuple((jnp.expand_dims(member, axis_dim) for member in down_in)), down_local)
    return (up_in, up_whole, down_in, down_whole)


def open_edge(conduct, axis_dim, position):
    span = conduct.shape[axis_dim]
    place = lax.broadcasted_iota(jnp.int32, conduct.shape, axis_dim) + position * span
    return jnp.where(place == 0, jnp.zeros_like(conduct), conduct)


def operator_terms(kleft, axis_dim, across):
    span = kleft.shape[axis_dim]
    matrices = (1.0 + kleft, kleft, jnp.ones_like(kleft), kleft)
    up_in, up_whole, down_in, down_whole = chain(matrices, matrices, mobius_join, axis_dim, across)
    after = mobius_value(up_whole)
    before = jnp.concatenate(
        [
            jnp.expand_dims(mobius_value(up_in), axis_dim),
            lax.slice_in_dim(after, 0, span - 1, 1, axis_dim),
        ],
        axis_dim,
    )
    behind_whole = mobius_value(down_whole)
    behind = jnp.concatenate(
        [
            lax.slice_in_dim(behind_whole, 1, span, 1, axis_dim),
            jnp.expand_dims(mobius_value(down_in), axis_dim),
        ],
        axis_dim,
    )
    return (kleft / (before + kleft), kleft / (behind + kleft), after + behind - 1.0)


def line_solve(values, terms, axis_dim, across):
    forward_rate, backward_rate, diagonal = terms
    span = values.shape[axis_dim]
    up_in, up_whole, down_in, down_whole = chain(
        (forward_rate, values),
        (backward_rate, backward_rate * values),
        affine_join,
        axis_dim,
        across,
    )
    passed = down_whole[1]
    passed_next = jnp.concatenate(
        [lax.slice_in_dim(passed, 1, span, 1, axis_dim), jnp.expand_dims(down_in[1], axis_dim)],
        axis_dim,
    )
    return (up_whole[1] + passed_next) / diagonal


def to_lines(field, partners):
    row_count = field.shape[0]
    flattened = field.reshape(row_count, -1)
    padding = -flattened.shape[1] % partners
    return jnp.pad(flattened, ((0, 0), (0, padding)))


def from_lines(lines, target_shape):
    return lines[:, : target_shape[1] * target_shape[2]].reshape(target_shape)


def body(chi, sigma, vertical, kx, ky):
    fields = vertical.shape[0]
    levels = vertical.shape[1]
    width = fields * levels
    scaled = sigma * chi
    blocks = (
        jnp.eye(fields, dtype=jnp.float32)[:, None, :, None] * vertical[:, :, None, :]
    ).reshape(width, width)
    mixed = jnp.dot(scaled.reshape(-1, width), blocks, precision=lax.Precision.HIGHEST).reshape(
        scaled.shape
    )
    x_terms = operator_terms(open_edge(kx, 1, lax.axis_index("gx")), 1, across_x)
    partners = lax.axis_size("gy")
    whole_conduct = lax.all_to_all(
        to_lines(ky, partners), "gy", split_axis=1, concat_axis=0, tiled=True
    )
    y_terms = operator_terms(open_edge(whole_conduct, 0, 0), 0, across_y)
    current = mixed
    for sweep in range(ITERS):
        current = line_solve(current, x_terms, 1, across_x)
        whole_lines = lax.all_to_all(
            to_lines(current, partners), "gy", split_axis=1, concat_axis=0, tiled=True
        )
        solved = line_solve(whole_lines, y_terms, 0, across_y)
        current = from_lines(
            lax.all_to_all(solved, "gy", split_axis=0, concat_axis=1, tiled=True), current.shape
        )
    return current


LANES = 128
SUBLANES = 8


def channels_fit(shape, fields, split_x, split_y):
    rows, span, width = shape
    return (
        span == SUBLANES
        and rows * span * split_x == LANES
        and fields == split_x
        and SUBLANES % split_x == 0
        and width == SUBLANES * split_x * split_y
        and rows & (rows - 1) == 0
        and split_x & (split_x - 1) == 0
        and split_y & (split_y - 1) == 0
    )


def cyclic_reduction(kleft, length, at, paired, values):
    excess = jnp.ones_like(kleft)
    west = kleft
    east = at(kleft, 1)
    levels = []
    stride = 1
    while stride < length:
        inverse = 1.0 / (excess + west + east)
        from_west = west * at(inverse, -stride)
        from_east = east * at(inverse, stride)
        excess = excess + from_west * at(excess, -stride) + from_east * at(excess, stride)
        west = from_west * at(west, -stride)
        east = from_east * at(east, stride)
        levels.append((stride, from_west, from_east))
        if values is not None:
            values = values + (from_west * at(values, -stride) + from_east * at(values, stride))
        stride *= 2
    inverse = 1.0 / excess
    if values is not None:
        values = values * inverse
    steps = []
    while levels:
        near, west_near, east_near = levels.pop(0)
        if levels and paired(near):
            far, west_far, east_far = levels.pop(0)
            steps.append(
                (
                    (-near, west_near + west_far * at(east_near, -far)),
                    (near, east_near + east_far * at(west_near, far)),
                    (-far, west_far),
                    (far, east_far),
                    (-near - far, west_far * at(west_near, -far)),
                    (near + far, east_far * at(east_near, far)),
                )
            )
        else:
            steps.append(((-near, west_near), (near, east_near)))
    return (steps, inverse), values


def reduced_solve(values, operator, at):
    steps, inverse = operator
    for taps in steps:
        terms = [coefficient * at(values, offset) for offset, coefficient in taps]
        terms = [first + second for first, second in zip(terms[::2], terms[1::2])]
        values = (values + terms[0]) + sum(terms[2:], terms[1]) if terms[1:] else values + terms[0]
    return values * inverse


def swap_blocks(values, span, split_x):
    share = SUBLANES // split_x
    tiles = values.reshape(-1, SUBLANES, LANES)
    group = lax.broadcasted_iota(jnp.int32, tiles.shape, 1) // share
    block = (lax.broadcasted_iota(jnp.int32, tiles.shape, 2) // span) % split_x
    apart = (block - group + split_x) % split_x
    swapped = tiles
    for k in range(1, split_x):
        ahead = pltpu.roll(tiles, span * k, 2)
        wrapped = pltpu.roll(tiles, LANES - span * (split_x - k), 2)
        moved = pltpu.roll(jnp.where(block >= k, ahead, wrapped), SUBLANES - share * k, 1)
        swapped = jnp.where(apart == k, moved, swapped)
    return swapped.reshape(values.shape)


def channel_kernel(
    split_x,
    split_y,
    chi_hbm,
    sigma_hbm,
    vertical_hbm,
    kx_hbm,
    ky_hbm,
    out_ref,
    chi_ref,
    sigma_ref,
    vertical_ref,
    kx_ref,
    ky_ref,
    sent,
    got,
    solved,
    back,
    load_sems,
    sems,
    back_sems,
):
    rows, span, width = chi_ref.shape
    fields, levels, _ = vertical_ref.shape
    count = split_x * split_y
    length_x = split_x * span
    length_y = split_y * rows
    tall = split_y * SUBLANES
    gx, gy = (lax.axis_index("gx"), lax.axis_index("gy"))
    me = gy * split_x + gx

    loads = [
        pltpu.make_async_copy(source, target, load_sems.at[number])
        for number, (source, target) in enumerate(
            (
                (kx_hbm, kx_ref),
                (ky_hbm, ky_ref),
                (chi_hbm, chi_ref),
                (sigma_hbm, sigma_ref),
                (vertical_hbm, vertical_ref),
            )
        )
    ]
    for load in loads:
        load.start()

    partners_x = [lax.bitwise_xor(gx, jnp.int32(step)) for step in range(split_x)]
    partners_y = [lax.bitwise_xor(gy, jnp.int32(step)) for step in range(split_y)]
    partners = [
        (partners_x[step_x], partners_y[step_y])
        for step_y in reversed(range(split_y))
        for step_x in reversed(range(split_x))
        if step_x or step_y
    ]

    barrier = pltpu.get_barrier_semaphore()
    for peer_x, peer_y in partners:
        pl.semaphore_signal(
            barrier,
            inc=1,
            device_id={"gx": peer_x, "gy": peer_y},
            device_id_type=pl.DeviceIdType.MESH,
        )

    def send_all(source, target, sems):
        for peer_x, peer_y in partners:
            pltpu.make_async_remote_copy(
                src_ref=source(peer_y * split_x + peer_x),
                dst_ref=target(me),
                send_sem=sems.at[0],
                recv_sem=sems.at[1],
                device_id={"gx": peer_x, "gy": peer_y},
                device_id_type=pl.DeviceIdType.MESH,
            ).start()

    others = pl.ds(0, count - 1)
    loads[0].wait()
    loads[1].wait()
    group = width // split_x
    conducts = jnp.concatenate(
        [
            jnp.concatenate([ref[row][:, h * group : (h + 1) * group] for ref in (kx_ref, ky_ref)], 1)
            for row in range(rows)
            for h in range(split_x)
        ],
        0,
    )
    conducts = conducts.T.reshape((2,) + back.shape)
    sent[:, 0] = conducts[0]
    sent[:, 1] = conducts[1]

    for load in loads[2:]:
        load.wait()
    field_of = lax.broadcasted_iota(jnp.int32, (span, width), 1) // levels
    scaled = [sigma_ref[row] * chi_ref[row] for row in range(rows)]
    stacked = jnp.dot(
        jnp.concatenate(
            [jnp.where(field_of == f, scaled[row], 0.0) for row in range(rows) for f in range(fields)],
            0,
        ),
        vertical_ref[...].reshape(width, levels),
        precision=lax.Precision.HIGHEST,
        preferred_element_type=jnp.float32,
    )
    sent[:, 2] = stacked.T.reshape(back.shape)
    pl.semaphore_wait(barrier, count - 1)
    send_all(lambda at: sent.at[at], lambda at: got.at[at], sems)
    got[me] = sent[me]

    lane = lax.broadcasted_iota(jnp.int32, (tall, LANES), 1)
    tile_row = lax.broadcasted_iota(jnp.int32, (tall, LANES), 0)
    cell_x = lane % length_x

    def tiles_on(values, tiles_by):
        moved = (tiles_by % split_y) * SUBLANES
        if moved == 0:
            return values
        return jnp.concatenate([values[-moved:], values[:-moved]], 0)

    def at_x(values, offset):
        return pltpu.roll(values, (LANES - offset) % LANES, 1)

    def at_y(values, offset):
        if abs(offset) >= rows:
            return tiles_on(values, -offset // rows)
        lanes = offset * length_x
        turned_by = pltpu.roll(values, (LANES - lanes) % LANES, 1)
        if offset < 0:
            return jnp.where(lane < -lanes, tiles_on(turned_by, 1), turned_by)
        return jnp.where(lane >= LANES - lanes, tiles_on(turned_by, -1), turned_by)

    pltpu.make_async_copy(got.at[others], got.at[others], sems.at[1]).wait()
    west = swap_blocks(got[:, 0].reshape(tall, LANES), span, split_x)
    south = swap_blocks(got[:, 1].reshape(tall, LANES), span, split_x)
    west = jnp.where(cell_x == 0, 0.0, west)
    south = jnp.where((tile_row < SUBLANES) & (lane < length_x), 0.0, south)
    field = swap_blocks(got[:, 2].reshape(tall, LANES), span, split_x)
    x_operator, field = cyclic_reduction(
        west, length_x, at_x, lambda near: 3 * near < length_x, field
    )
    y_operator, _ = cyclic_reduction(south, length_y, at_y, lambda near: 3 * near < rows, None)
    for sweep in range(ITERS):
        if sweep:
            field = reduced_solve(field, x_operator, at_x)
        field = reduced_solve(field, y_operator, at_y)
    solved[...] = swap_blocks(field, span, split_x).reshape(solved.shape)
    send_all(lambda at: solved.at[at], lambda at: back.at[at], back_sems)
    back[me] = solved[me]
    pltpu.make_async_copy(back.at[others], back.at[others], back_sems.at[1]).wait()
    turned = back[...].reshape(tall, LANES).T
    for row in range(rows):
        out_ref[row] = jnp.concatenate(
            [
                turned[(row * split_x + h) * span : (row * split_x + h + 1) * span]
                for h in range(split_x)
            ],
            1,
        )
    pltpu.make_async_copy(sent.at[others], sent.at[others], sems.at[0]).wait()
    pltpu.make_async_copy(solved.at[others], solved.at[others], back_sems.at[0]).wait()


def channel_body(split_x, split_y, chi, sigma, vertical, kx, ky):
    count = split_x * split_y
    share = SUBLANES // split_x
    block = pltpu.VMEM(chi.shape, jnp.float32)
    packed = pltpu.VMEM((count, share, LANES), jnp.float32)
    packed_triple = pltpu.VMEM((count, 3, share, LANES), jnp.float32)
    return pl.pallas_call(
        functools.partial(channel_kernel, split_x, split_y),
        out_shape=pltpu.VMEM(chi.shape, jnp.float32),
        in_specs=[pl.BlockSpec(memory_space=pl.ANY)] * 5,
        out_specs=pl.BlockSpec(memory_space=pltpu.VMEM),
        scratch_shapes=[
            block,
            block,
            pltpu.VMEM(vertical.shape, jnp.float32),
            block,
            block,
            packed_triple,
            packed_triple,
            packed,
            packed,
            pltpu.SemaphoreType.DMA((5,)),
            pltpu.SemaphoreType.DMA((2,)),
            pltpu.SemaphoreType.DMA((2,)),
        ],
        compiler_params=pltpu.CompilerParams(collective_id=0, has_side_effects=True),
        name="channel_lines",
    )(chi, sigma, vertical, kx, ky)


def solution(mesh):
    split_x, split_y = (mesh.shape["gx"], mesh.shape["gy"])

    def chosen(chi, sigma, vertical, kx, ky):
        if channels_fit(chi.shape, vertical.shape[0], split_x, split_y):
            return channel_body(split_x, split_y, chi, sigma, vertical, kx, ky)
        return body(chi, sigma, vertical, kx, ky)


    placed = (
        P("gy", "gx", None),
        P("gy", "gx", None),
        P(),
        P("gy", "gx", None),
        P("gy", "gx", None),
    )
    return jax.shard_map(
        chosen, mesh=mesh, in_specs=placed, out_specs=P("gy", "gx", None), check_vma=False
    )
```
